32 devices in a mesh: src: 16 (over z, x, core), tm: 2 (over y).
Axes of the slice: x: 2, y: 2, z: 4, core: 2. Of those that a mesh axis runs over, the one named last changes fastest.
Arguments:
- left_vector: float32 [2, 8192], P(None, ('src', 'tm')), may hold values from -12 to 12
- source_coeffs: float32 [5, 2, 8192], P(None, None, ('src', 'tm')), may hold values from -1.5 to 1.5
- knot_coeffs: float32 [12, 2, 8192], P(None, None, ('src', 'tm')), may hold values from -1.5 to 1.5
- source_index: int32 [2, 8192], P(None, ('src', 'tm')), may hold values from 0 to 1023
- band_start: int32 [2, 8192], P(None, ('src', 'tm')), may hold values from 0 to 1023, as said below
- bucket_fill: int32 [2, 32], P(None, ('src', 'tm')), may hold values from 51 to 256, as said below
- source_vector: float32 [5, 32768], P(None, ('src', 'tm')), may hold values from -6 to 6
- knot_vector: float32 [3, 2, 4096], P(None, 'tm', 'src'), may hold values from -6 to 6
- source_search: float32 [5, 32768], P(None, ('src', 'tm')), may hold values from -6 to 6
- knot_search: float32 [3, 2, 4096], P(None, 'tm', 'src'), may hold values from -6 to 6
- source_solution: float32 [5, 32768], P(None, ('src', 'tm')), may hold values from -6 to 6
- knot_solution: float32 [3, 2, 4096], P(None, 'tm', 'src'), may hold values from -6 to 6
- recurrence: float32 [3], replicated, may hold values from 0.5 to 1.5
Outputs:
- left_next: float32 [2, 8192], P(None, ('src', 'tm'))
- source_next: float32 [5, 32768], P(None, ('src', 'tm'))
- knot_next: float32 [3, 2, 4096], P(None, 'tm', 'src')
- search_source: float32 [5, 32768], P(None, ('src', 'tm'))
- search_knot: float32 [3, 2, 4096], P(None, 'tm', 'src')
- solution_source: float32 [5, 32768], P(None, ('src', 'tm'))
- solution_knot: float32 [3, 2, 4096], P(None, 'tm', 'src')
- recurrence_next: float32 [4], replicated
The draws below stay inside these ranges and needn't reach their ends.
Inputs may be any that keep to these rules, and one draw needn't show every extreme that they name: `bucket_fill`: in every draw one bucket of some group block holds exactly 256 observations. Call band_start // 64 the knot owner of a slot. Among the 2 x 256 slots of one column block of 256, each knot owner is named at most 64 times, and in every block some owner exactly 64 times.
All inputs are finite; a program needn't handle non-finite values.
Results may differ from the reference program's by a relative error of at most 0.00002.
Values sent between devices are 32-bit elements; how exact they have to be, the bound alone decides.
No kernel may reach another device: no remote copies, remote signals or barrier semaphores. Data moves between devices by JAX's collectives and lax.ppermute only.
A program may use at most 64 MiB of HBM per device.

```python
import jax
import jax.numpy as jnp
from jax import lax

SRC_DEV = 1024
CAP = 256
KNOT_DEV = 256
KB = 4
SOURCES = 32768
NOBS_COL = 8192
KNOTS_SLAB = 4096
N_SRC = 16
N_TM = 2


def draw_left_vector(key, part):
    blocks = NOBS_COL // CAP
    rank = (jnp.arange(NOBS_COL) // CAP).astype(jnp.float32) / max(blocks - 1, 1)
    base = jax.random.normal(key, (N_TM, NOBS_COL), jnp.float32)
    scale = 1.0 + 2.0 * rank
    values = base * scale[None, :]
    return jnp.clip(values, -12.0, 12.0)


def draw_bucket_fill(key, part):
    blocks = NOBS_COL // CAP
    fill = jax.random.randint(key, (N_TM * blocks,), CAP // 5, CAP + 1)
    chosen = jax.random.randint(jax.random.fold_in(key, 7), (), 0, N_TM * blocks)
    fill = jnp.where(jnp.arange(N_TM * blocks) == chosen, CAP, fill)
    return fill.reshape(N_TM, blocks).astype(jnp.int32)


def band_block(block_key):
    local_slots = N_TM * CAP
    half_most = local_slots // N_SRC
    bands_owner = KNOT_DEV // KB
    key_slots, key_owner, key_coin, key_band = jax.random.split(block_key, 4)
    bucket = jax.random.permutation(key_slots, local_slots) // half_most
    owners = jax.random.permutation(key_owner, N_SRC)
    coins = jax.random.randint(key_coin, (N_SRC,), 0, 2)
    coins = coins.at[0].set(1).at[1].set(0)
    target = jnp.where(coins[bucket] == 1, owners[(bucket + 1) % N_SRC], owners[bucket])
    local_band = jax.random.randint(key_band, (local_slots,), 0, bands_owner)
    return (target * bands_owner + local_band).astype(jnp.int32).reshape(N_TM, CAP)


def draw_band_start(key, part):
    blocks = NOBS_COL // CAP
    block_keys = jax.random.split(jax.random.fold_in(key, 11), blocks)
    drawn = jax.vmap(band_block)(block_keys)
    return jnp.transpose(drawn, (1, 0, 2)).reshape(N_TM, NOBS_COL).astype(jnp.int32)


def place_ends(values, own_key, smallest, high):
    spot = [jax.random.randint(jax.random.fold_in(own_key, axis), (), 0, length) for axis, length in enumerate(values.shape)]
    longest = values.shape.index(max(values.shape))
    next_to = spot[:longest] + [(spot[longest] + 1) % values.shape[longest]] + spot[longest + 1:]
    return values.at[tuple(spot)].set(smallest).at[tuple(next_to)].set(high)


def level_of(own_key, extent, pieces, least, high):
    factor_of = 1.0
    for position, blocks in pieces:
        draws = jax.random.uniform(jax.random.fold_in(jax.random.fold_in(own_key, 6), position), (blocks,), jnp.float32, least / len(pieces), high / len(pieces))
        factor_of = factor_of * jnp.repeat(jnp.exp(draws), extent[position] // blocks).reshape((-1,) + (1,) * (len(extent) - 1 - position))
    return factor_of


def gaussian(rng, shape, deviation, reach, shards=(), held_as=jnp.bfloat16):
    values = deviation * jax.random.normal(rng, shape, jnp.float32)
    if shards:
        values = values * level_of(rng, shape, shards, -0.22, 0.18)
    return jnp.clip(values, -reach, reach).astype(held_as)


def setup_inputs(seed: int = 0) -> dict:
    streams_of = jax.random.split(jax.random.key(seed), 14)
    return {
        "left_vector": draw_left_vector(jax.random.fold_in(streams_of[13], 71), 0),
        "source_coeffs": gaussian(streams_of[1], (5, N_TM, NOBS_COL), 0.25, 1.5, ((2, 32),), jnp.float32),
        "knot_coeffs": gaussian(streams_of[2], (3 * KB, N_TM, NOBS_COL), 0.25, 1.5, ((2, 32),), jnp.float32),
        "source_index": place_ends(jax.random.randint(streams_of[3], (N_TM, NOBS_COL), 0, SRC_DEV), jax.random.fold_in(streams_of[3], 1), 0, SRC_DEV - 1).astype(jnp.int32),
        "band_start": draw_band_start(jax.random.fold_in(streams_of[13], 71), 0),
        "bucket_fill": draw_bucket_fill(jax.random.fold_in(streams_of[13], 71), 0),
        "source_vector": gaussian(streams_of[6], (5, SOURCES), 1.0, 6.0, ((1, 32),), jnp.float32),
        "knot_vector": gaussian(streams_of[7], (3, N_TM, KNOTS_SLAB), 1.0, 6.0, ((1, 2), (2, 16)), jnp.float32),
        "source_search": gaussian(streams_of[8], (5, SOURCES), 1.0, 6.0, ((1, 32),), jnp.float32),
        "knot_search": gaussian(streams_of[9], (3, N_TM, KNOTS_SLAB), 1.0, 6.0, ((1, 2), (2, 16)), jnp.float32),
        "source_solution": gaussian(streams_of[10], (5, SOURCES), 1.0, 6.0, ((1, 32),), jnp.float32),
        "knot_solution": gaussian(streams_of[11], (3, N_TM, KNOTS_SLAB), 1.0, 6.0, ((1, 2), (2, 16)), jnp.float32),
        "recurrence": jnp.clip(jax.random.uniform(streams_of[12], (3,), jnp.float32, 0.5, 1.5), 0.5, 1.5),
    }


EPSILON = 1e-06

def regroup(values):
    shaped = values.reshape(N_TM, N_SRC, N_TM, CAP)
    return jnp.transpose(shaped, (2, 1, 0, 3)).reshape(N_TM, NOBS_COL)

def reference(left_vector, source_coeffs, knot_coeffs, source_index, band_start, bucket_fill, source_vector, knot_vector, source_search, knot_search, source_solution, knot_solution, recurrence):
    total_obs = N_TM * NOBS_COL
    unknowns = 5 * SOURCES + 3 * N_TM * KNOTS_SLAB
    ratio = unknowns / total_obs
    alpha = recurrence[0]
    pivot = recurrence[1]
    remainder = recurrence[2]
    column = lax.broadcasted_iota(jnp.int32, (N_TM, NOBS_COL), 1)
    block = column // CAP
    valid = (column % CAP < jnp.repeat(bucket_fill, CAP, axis=1)).astype(jnp.float32)
    source_of = (block * SRC_DEV + source_index).astype(jnp.int32)
    slab_of = (block % N_TM).astype(jnp.int32)
    first_knot = (band_start * KB).astype(jnp.int32)
    image = jnp.zeros((N_TM, NOBS_COL), jnp.float32)
    for k in range(5):
        image = image + source_coeffs[k] * source_vector[k][source_of]
    knot_image = jnp.zeros((N_TM, NOBS_COL), jnp.float32)
    for row in range(3 * KB):
        axis_id = row // KB
        offset = row % KB
        knot_image = knot_image + knot_coeffs[row] * knot_vector[axis_id][slab_of, (first_knot + offset).astype(jnp.int32)]
    raw = valid * (image + regroup(knot_image) - alpha * left_vector)
    beta = jnp.sqrt(jnp.sum(raw * raw) / total_obs + EPSILON)
    left_next = raw / beta
    left_slab = regroup(left_next)
    gradient_source = jnp.zeros((5, SOURCES), jnp.float32).at[:, source_of.reshape(-1)].add((source_coeffs * left_next[None]).reshape(5, -1))
    gradient_knot = jnp.zeros((3, N_TM, KNOTS_SLAB), jnp.float32)
    for row in range(3 * KB):
        axis_id = row // KB
        offset = row % KB
        gradient_knot = gradient_knot.at[axis_id, slab_of, (first_knot + offset).astype(jnp.int32)].add(knot_coeffs[row] * left_slab)
    source_raw = ratio * gradient_source - beta * source_vector
    knot_raw = ratio * gradient_knot - beta * knot_vector
    alpha_next = jnp.sqrt((jnp.sum(source_raw * source_raw) + jnp.sum(knot_raw * knot_raw)) / unknowns + EPSILON)
    source_next = source_raw / alpha_next
    knot_next = knot_raw / alpha_next
    radius = jnp.sqrt(pivot * pivot + beta * beta)
    cosine = pivot / radius
    sine = beta / radius
    coupling = sine * alpha_next
    step_gain = cosine * remainder
    solution_source = source_solution + step_gain / radius * source_search
    solution_knot = knot_solution + step_gain / radius * knot_search
    search_source = source_next - coupling / radius * source_search
    search_knot = knot_next - coupling / radius * knot_search
    recurrence_next = jnp.stack([alpha_next, beta, -cosine * alpha_next, sine * remainder])
    return (left_next, source_next, knot_next, search_source, search_knot, solution_source, solution_knot, recurrence_next)
```

```python
import functools

import jax
import jax.numpy as jnp
from jax import lax
from jax.experimental import pallas as pl
from jax.experimental.pallas import tpu as pltpu
from jax.sharding import PartitionSpec as P

KB = 4
ROWS = 3 * KB
LANES = 128
EPSILON = 1e-06
F32 = jnp.float32
BF16 = jnp.bfloat16
I32 = jnp.int32


def iota(shape, axis):
    return lax.broadcasted_iota(I32, shape, axis)


def split3(x):
    hi = x.astype(BF16).astype(F32)
    rest = x - hi
    mid = rest.astype(BF16).astype(F32)
    return jnp.concatenate([hi, mid, rest - mid], axis=0).astype(BF16)


def fold3(y):
    n = y.shape[0] // 3
    return (y[2 * n :] + y[n : 2 * n]) + y[:n]


def dot(a, b):
    return lax.dot_general(a, b, (((1,), (0,)), ((), ())), preferred_element_type=F32)


def dot_nt(a, b):
    return lax.dot_general(a, b, (((1,), (1,)), ((), ())), preferred_element_type=F32)


def pick(values, onehot):
    return fold3(dot(split3(values), onehot))


def put(values, onehot):
    return fold3(dot_nt(split3(values), onehot))


def onehot(count, index):
    hit = iota((count, index.shape[1]), 0) == index
    return jnp.where(hit, 1.0, 0.0).astype(BF16)


def pad_rows(x, n):
    return jnp.concatenate([x, jnp.zeros((n - x.shape[0], x.shape[1]), F32)], axis=0)


def row_parts(shape):
    row = iota(shape, 0)
    upper = (row >= 8).astype(I32)
    held = (row - 8 * upper) < ROWS // 2
    c = row - 2 * upper
    return held, c >> 2, c & (KB - 1)


def halves(x, low):
    return jnp.where(low, x[:8], x[8:])


def before_kernel(groups, slabs, source_index, source_coeffs, source_vector, left, fill, recurrence, knot_coeffs, band, knots, send, partial_out, own):
    buckets, capacity = left.shape
    source_dev = source_vector.shape[1]
    knot_dev = knots.shape[2]
    bands = knot_dev // KB
    shift = bands.bit_length() - 1
    alpha = recurrence[0]
    low8 = iota((8, LANES), 1) < bands
    slot = iota((1, capacity), 1)

    vector = split3(pad_rows(source_vector[...], 8))
    partial = []
    for t in range(buckets):
        hot = onehot(source_dev, source_index[pl.ds(t, 1), :])
        picked = fold3(dot(vector, hot))[:5]
        image = jnp.sum(source_coeffs[:, t, :] * picked, axis=0, keepdims=True)
        partial.append(jnp.where(slot < fill[t, 0], image - alpha * left[pl.ds(t, 1), :], 0.0))
        partial_out[pl.ds(t, 1), :] = partial[t]

    total = jnp.zeros((groups, 1), F32)
    before = jnp.where(iota((capacity, capacity), 0) < iota((capacity, capacity), 1), 1.0, 0.0).astype(BF16)
    packed = jnp.zeros((16, groups * bands), F32)
    for i in range(buckets):
        bands_i = band[pl.ds(i, 1), :]
        owner = bands_i >> shift
        named = jnp.where(iota((groups, capacity), 0) == owner, 1.0, 0.0)
        count = dot(named.astype(BF16), before) + total
        rank = jnp.sum(named * count, axis=0, keepdims=True).astype(I32)
        total = total + jnp.sum(named, axis=1, keepdims=True)
        hot = onehot(groups * bands, owner * bands + rank)
        local = (bands_i - owner * bands).astype(F32)
        place = (slot + i * capacity).astype(F32)
        zero = jnp.zeros((1, capacity), F32)
        coeffs = knot_coeffs[:, i, :]
        values = jnp.concatenate([coeffs[: ROWS // 2], local, zero, coeffs[ROWS // 2 :], place, zero], axis=0)
        packed = packed + put(values, hot)

    held, axis_of, offset = row_parts((16, knot_dev))
    spread = jnp.zeros((16, knot_dev), F32)
    for a in range(3):
        spread = jnp.where(axis_of == a, knots[a], spread)
    spread = jnp.where(held & ((iota((16, knot_dev), 1) & (KB - 1)) == offset), spread, 0.0)
    hit = (iota((knot_dev, LANES), 0) >> 2) == (iota((knot_dev, LANES), 1) & (bands - 1))
    rows = pick(spread, jnp.where(hit, 1.0, 0.0).astype(BF16))
    own[...] = rows
    knot_rows = halves(rows, low8)[: ROWS // 2]

    last = iota((8, LANES), 0) == 7
    first = [
        jnp.concatenate([knot_rows] + [partial[t][:, k * LANES : (k + 1) * LANES] for k in range(2)], axis=0)
        for t in range(buckets)
    ]
    for g in range(groups // 2):
        tile = packed[:, g * LANES : (g + 1) * LANES]
        turned = pltpu.roll(tile, bands, 1)
        pair = (jnp.where(low8, tile[:8], turned[8:]), jnp.where(low8, turned[:8], tile[8:]))
        for h in range(2):
            for t in range(slabs):
                block = (2 * g + h) * slabs + t
                send[block, 0:8, :] = first[t]
                send[block, 8:16, :] = jnp.where(last, fill[t, 0].astype(F32), pair[h])


def joined(even, odd, low, bands):
    return jnp.concatenate(
        [jnp.where(low, even, pltpu.roll(odd, bands, 1)), jnp.where(low, pltpu.roll(even, bands, 1), odd)], axis=0
    )


def middle_kernel(groups, slabs, recv, exchanged, partial, left, fill, recurrence, source_index, source_coeffs, source_vector, knots, own, raw_out, gradient_source, gradient_knot, sums):
    buckets, capacity = left.shape
    source_dev = source_vector.shape[1]
    knot_dev = knots.shape[2]
    bands = knot_dev // KB
    shift = bands.bit_length() - 1
    capacity_shift = capacity.bit_length() - 1
    devices = groups * slabs
    packets = groups * bands
    alpha = recurrence[0]
    my_slab = lax.axis_index("tm")
    low = iota((8, LANES), 1) < bands
    slot = iota((1, capacity), 1)

    gathered_sum = jnp.zeros((8, source_dev), F32)
    squares = jnp.zeros((1, capacity), F32)
    cross = jnp.zeros((1, capacity), F32)
    for t in range(buckets):
        table = jnp.concatenate(
            [
                joined(recv[2 * g * slabs + t, 0:8, :], recv[(2 * g + 1) * slabs + t, 0:8, :], low, bands)
                for g in range(groups // 2)
            ],
            axis=1,
        )
        block = exchanged[t]
        coeffs = jnp.concatenate(
            [pad_rows(block[: ROWS // 2], 8), pad_rows(block[ROWS // 2 : ROWS], 8)], axis=0
        )
        hot = onehot(packets, block[ROWS : ROWS + 1].astype(I32))
        image = jnp.sum(coeffs * pick(table, hot), axis=0, keepdims=True)
        raw = partial[pl.ds(t, 1), :] + jnp.where(slot < fill[t, 0], image, 0.0)
        raw_out[pl.ds(t, 1), :] = raw
        squares = squares + raw * raw
        cross = cross + raw * (raw + alpha * left[pl.ds(t, 1), :])
        hot = onehot(source_dev, source_index[pl.ds(t, 1), :])
        gathered_sum = gathered_sum + put(pad_rows(source_coeffs[:, t, :] * raw, 8), hot)
    gradient_source[...] = gathered_sum[:5]

    packet = jnp.concatenate(
        [
            joined(
                recv[2 * g * slabs + my_slab, 8:16, :], recv[(2 * g + 1) * slabs + my_slab, 8:16, :], low, bands
            )
            for g in range(groups // 2)
        ],
        axis=1,
    )
    band = packet[6:7].astype(I32)
    place = packet[14:15].astype(I32)
    inner = place & (capacity - 1)
    sender = (iota((1, packets), 1) >> shift) * slabs + (place >> capacity_shift)
    chosen = iota((devices, packets), 0) == sender
    partials = jnp.concatenate([recv[:, 6, :], recv[:, 7, :]], axis=1)
    found = pick(partials, onehot(capacity, inner))
    fills = jnp.concatenate([recv[:, 15, :]] * (packets // LANES), axis=1)
    partial_packet = jnp.sum(jnp.where(chosen, found, 0.0), axis=0, keepdims=True)
    fill_packet = jnp.sum(jnp.where(chosen, fills, 0.0), axis=0, keepdims=True)
    hot = onehot(bands, band)
    image = jnp.sum(packet * pick(own[...][:, :bands], hot), axis=0, keepdims=True)
    raw = jnp.where(inner.astype(F32) < fill_packet, partial_packet + image, 0.0)
    collected = put(packet * raw, hot)
    hit = iota((bands, knot_dev), 0) == (iota((bands, knot_dev), 1) >> 2)
    spread = pick(collected, jnp.where(hit, 1.0, 0.0).astype(BF16))
    held, axis_of, offset = row_parts((16, knot_dev))
    spread = jnp.where(held & ((iota((16, knot_dev), 1) & (KB - 1)) == offset), spread, 0.0)
    knot_squares = jnp.zeros((1, knot_dev), F32)
    knot_old = jnp.zeros((1, knot_dev), F32)
    for a in range(3):
        total = jnp.sum(jnp.where(axis_of == a, spread, 0.0), axis=0, keepdims=True)
        gradient_knot[a] = total
        knot_squares = knot_squares + total * total
        knot_old = knot_old + knots[a] * knots[a]

    own_squares = jnp.sum(squares)
    cross_sum = jnp.sum(cross)
    gradient_squares = jnp.sum(gathered_sum * gathered_sum) + jnp.sum(knot_squares)
    old = source_vector[...]
    old_squares = jnp.sum(old * old) + jnp.sum(knot_old)
    lane = iota((devices, LANES), 1)
    sums[...] = jnp.where(
        lane == 0,
        own_squares,
        jnp.where(lane == 1, gradient_squares, jnp.where(lane == 2, cross_sum, old_squares)),
    )


def after_kernel(total_obs, unknowns, sums, recurrence, raw, gradient_source, gradient_knot, source_vector, knots, source_search, knot_search, source_solution, knot_solution, left_next, source_next, knot_next, search_source, search_knot, solution_source, solution_knot, recurrence_next):
    ratio = unknowns / total_obs
    pivot = recurrence[1]
    remainder = recurrence[2]
    total = jnp.sum(sums[...], axis=0, keepdims=True)
    s0, s1, s2, s3 = (total[:, k : k + 1] for k in range(4))
    beta = jnp.sqrt(s0 / total_obs + EPSILON)
    scaled = ratio / beta
    alpha_square = scaled * scaled * s1 - 2.0 * ratio * s2 + beta * beta * s3
    alpha_next = jnp.sqrt(alpha_square / unknowns + EPSILON)
    radius = jnp.sqrt(pivot * pivot + beta * beta)
    cosine = pivot / radius
    sine = beta / radius
    gain = cosine * remainder / radius
    turn = sine * alpha_next / radius
    one_gradient = scaled / alpha_next
    one_vector = beta / alpha_next
    left_next[...] = raw[...] / beta
    search = source_search[...]
    value = one_gradient * gradient_source[...] - one_vector * source_vector[...]
    source_next[...] = value
    search_source[...] = value - turn * search
    solution_source[...] = source_solution[...] + gain * search
    for a in range(3):
        search = knot_search[a]
        value = one_gradient * gradient_knot[a] - one_vector * knots[a]
        knot_next[a] = value
        search_knot[a] = value - turn * search
        solution_knot[a] = knot_solution[a] + gain * search
    lane = iota((1, LANES), 1)
    recurrence_next[...] = jnp.where(
        lane == 0,
        alpha_next,
        jnp.where(lane == 1, beta, jnp.where(lane == 2, -cosine * alpha_next, sine * remainder)),
    )


VMEM = pl.BlockSpec(memory_space=pltpu.VMEM)
SMEM = pl.BlockSpec(memory_space=pltpu.SMEM)


def shards(
    left_vector,
    source_coeffs,
    knot_coeffs,
    source_index,
    band_start,
    bucket_fill,
    source_vector,
    knot_vector,
    source_search,
    knot_search,
    source_solution,
    knot_solution,
    recurrence,
):
    slabs = lax.axis_size("tm")
    groups = lax.axis_size("src")
    devices = slabs * groups
    buckets, capacity = left_vector.shape
    source_dev = source_vector.shape[1]
    knot_dev = knot_vector.shape[2]
    total_obs = buckets * capacity * devices
    unknowns = (5 * source_dev + 3 * knot_dev) * devices
    params = pltpu.CompilerParams(vmem_limit_bytes=48 * 1024 * 1024)
    shape = jax.ShapeDtypeStruct

    regroup = jnp.concatenate([knot_coeffs, band_start.astype(F32)[None]], axis=0)
    regroup = jnp.transpose(regroup, (1, 0, 2))
    exchanged = lax.all_to_all(regroup, "tm", split_axis=0, concat_axis=0, tiled=True)

    send, partial, own = pl.pallas_call(
        functools.partial(before_kernel, groups, slabs),
        out_shape=(
            shape((devices, 16, LANES), F32),
            shape((buckets, capacity), F32),
            shape((16, LANES), F32),
        ),
        in_specs=[VMEM, VMEM, VMEM, VMEM, SMEM, SMEM, VMEM, VMEM, VMEM],
        out_specs=(VMEM, VMEM, VMEM),
        compiler_params=params,
        name="before",
    )(
        source_index,
        source_coeffs,
        source_vector,
        left_vector,
        bucket_fill,
        recurrence,
        knot_coeffs,
        band_start,
        knot_vector,
    )
    recv = lax.all_to_all(send, ("src", "tm"), split_axis=0, concat_axis=0, tiled=True)
    raw, gradient_source, gradient_knot, sums = pl.pallas_call(
        functools.partial(middle_kernel, groups, slabs),
        out_shape=(
            shape((buckets, capacity), F32),
            shape((5, source_dev), F32),
            shape((3, 1, knot_dev), F32),
            shape((devices, LANES), F32),
        ),
        in_specs=[VMEM, VMEM, VMEM, VMEM, SMEM, SMEM, VMEM, VMEM, VMEM, VMEM, VMEM],
        out_specs=(VMEM, VMEM, VMEM, VMEM),
        compiler_params=params,
        name="middle",
    )(
        recv,
        exchanged,
        partial,
        left_vector,
        bucket_fill,
        recurrence,
        source_index,
        source_coeffs,
        source_vector,
        knot_vector,
        own,
    )
    sums = lax.all_to_all(sums, ("src", "tm"), split_axis=0, concat_axis=0, tiled=True)
    like = [shape(x.shape, F32) for x in (left_vector, source_vector, knot_vector)]
    outs = pl.pallas_call(
        functools.partial(after_kernel, total_obs, unknowns),
        out_shape=(like[0], like[1], like[2], like[1], like[2], like[1], like[2], shape((1, LANES), F32)),
        in_specs=[VMEM, SMEM] + [VMEM] * 9,
        out_specs=(VMEM,) * 8,
        compiler_params=params,
        name="after",
    )(
        sums,
        recurrence,
        raw,
        gradient_source,
        gradient_knot,
        source_vector,
        knot_vector,
        source_search,
        knot_search,
        source_solution,
        knot_solution,
    )
    return (*outs[:7], outs[7][0, :4])


def solution(mesh):
    wide = ("src", "tm")
    flat = P(None, wide)
    knot = P(None, "tm", "src")
    in_specs = (flat, P(None, None, wide), P(None, None, wide), flat, flat, flat, flat, knot, flat, knot, flat, knot, P())
    out_specs = (flat, flat, knot, flat, knot, flat, knot, P())
    return jax.shard_map(shards, mesh=mesh, in_specs=in_specs, out_specs=out_specs, check_vma=False)
```

```python
import functools

import jax
import jax.numpy as jnp
from jax import lax
from jax.experimental import pallas as pl
from jax.experimental.pallas import tpu as pltpu
from jax.sharding import PartitionSpec as P

KB = 4
ROWS = 3 * KB
LANES = 128
EPSILON = 1e-06
F32 = jnp.float32
BF16 = jnp.bfloat16
I32 = jnp.int32


def iota(shape, axis):
    return lax.broadcasted_iota(I32, shape, axis)


def split3(x):
    hi = x.astype(BF16).astype(F32)
    rest = x - hi
    mid = rest.astype(BF16).astype(F32)
    return jnp.concatenate([hi, mid, rest - mid], axis=0).astype(BF16)


def fold3(y):
    n = y.shape[0] // 3
    return (y[2 * n :] + y[n : 2 * n]) + y[:n]


def dot(a, b):
    return lax.dot_general(a, b, (((1,), (0,)), ((), ())), preferred_element_type=F32)


def dot_nt(a, b):
    return lax.dot_general(a, b, (((1,), (1,)), ((), ())), preferred_element_type=F32)


WIDE = 256


def pick(values, index):
    rows, count = values.shape
    width = min(count, WIDE)
    parts = count // width
    stacked = jnp.concatenate([values[:, h * width : (h + 1) * width] for h in range(parts)], axis=0)
    found = fold3(dot(split3(stacked), onehot(width, index & (width - 1))))
    high = index >> (width.bit_length() - 1)
    result = found[:rows]
    for h in range(1, parts):
        result = jnp.where(high == h, found[h * rows : (h + 1) * rows], result)
    return result


def put(values, index, count):
    rows = values.shape[0]
    width = min(count, WIDE)
    parts = count // width
    high = index >> (width.bit_length() - 1)
    if parts > 1:
        values = jnp.concatenate([jnp.where(high == h, values, 0.0) for h in range(parts)], axis=0)
    sums = fold3(dot_nt(split3(values), onehot(width, index & (width - 1))))
    return jnp.concatenate([sums[h * rows : (h + 1) * rows] for h in range(parts)], axis=1)


def onehot(count, index):
    hit = iota((count, index.shape[1]), 0) == index
    return jnp.where(hit, 1.0, 0.0).astype(BF16)


def pad_rows(x, n):
    return jnp.concatenate([x, jnp.zeros((n - x.shape[0], x.shape[1]), F32)], axis=0)


def row_parts(shape):
    row = iota(shape, 0)
    upper = (row >= 8).astype(I32)
    held = (row - 8 * upper) < ROWS // 2
    c = row - 2 * upper
    return held, c >> 2, c & (KB - 1)


def halves(x, low):
    return jnp.where(low, x[:8], x[8:])


def fetch(sources, targets, semaphores):
    copies = [pltpu.make_async_copy(a, b, semaphores.at[k]) for k, (a, b) in enumerate(zip(sources, targets))]
    for copy in copies:
        copy.start()
    return copies


def before_kernel(groups, slabs, *refs):
    count = 9
    sources, (send, partial_out, own) = refs[:count], refs[count : count + 3]
    targets, semaphores = refs[count + 3 : -1], refs[-1]
    for copy in fetch(sources, targets, semaphores):
        copy.wait()
    source_index, source_coeffs, source_vector, left, fill, recurrence, knot_coeffs, band, knots = targets
    buckets, capacity = left.shape
    source_dev = source_vector.shape[1]
    knot_dev = knots.shape[2]
    bands = knot_dev // KB
    shift = bands.bit_length() - 1
    alpha = recurrence[0]
    low8 = iota((8, LANES), 1) < bands
    slot = iota((1, capacity), 1)

    index = jnp.concatenate([source_index[pl.ds(t, 1), :] for t in range(buckets)], axis=1)
    picked = pick(pad_rows(source_vector[...], 8), index)[:5]
    partial = []
    for t in range(buckets):
        image = jnp.sum(source_coeffs[:, t, :] * picked[:, t * capacity : (t + 1) * capacity], axis=0, keepdims=True)
        partial.append(jnp.where(slot < fill[t], image - alpha * left[pl.ds(t, 1), :], 0.0))
        partial_out[pl.ds(t, 1), :] = partial[t]

    total = jnp.zeros((groups, 1), F32)
    before = jnp.where(iota((capacity, capacity), 0) < iota((capacity, capacity), 1), 1.0, 0.0).astype(BF16)
    targets, columns = [], []
    for i in range(buckets):
        bands_i = band[pl.ds(i, 1), :]
        owner = bands_i >> shift
        named = jnp.where(iota((groups, capacity), 0) == owner, 1.0, 0.0)
        count = dot(named.astype(BF16), before) + total
        rank = jnp.sum(named * count, axis=0, keepdims=True).astype(I32)
        total = total + jnp.sum(named, axis=1, keepdims=True)
        targets.append(owner * bands + rank)
        local = (bands_i - owner * bands).astype(F32)
        place = (slot + i * capacity).astype(F32)
        zero = jnp.zeros((1, capacity), F32)
        coeffs = knot_coeffs[:, i, :]
        columns.append(
            jnp.concatenate([coeffs[: ROWS // 2], local, zero, coeffs[ROWS // 2 :], place, zero], axis=0)
        )
    packed = put(jnp.concatenate(columns, axis=1), jnp.concatenate(targets, axis=1), groups * bands)

    held, axis_of, offset = row_parts((16, knot_dev))
    spread = jnp.zeros((16, knot_dev), F32)
    for a in range(3):
        spread = jnp.where(axis_of == a, knots[a], spread)
    spread = jnp.where(held & ((iota((16, knot_dev), 1) & (KB - 1)) == offset), spread, 0.0)
    hit = (iota((knot_dev, LANES), 0) >> 2) == (iota((knot_dev, LANES), 1) & (bands - 1))
    rows = fold3(dot(split3(spread), jnp.where(hit, 1.0, 0.0).astype(BF16)))
    own[0:16, :] = rows
    row, lane = iota((own.shape[0] - 16, LANES), 0), iota((own.shape[0] - 16, LANES), 1)
    scalars = jnp.where(lane == 0, alpha, jnp.where(lane == 1, recurrence[1], recurrence[2]))
    for t in range(buckets):
        scalars = jnp.where(row == 1 + t, fill[t].astype(F32), scalars)
    own[16:, :] = scalars
    knot_rows = halves(rows, low8)[: ROWS // 2]

    last = iota((8, LANES), 0) == 7
    first = [
        jnp.concatenate([knot_rows] + [partial[t][:, k * LANES : (k + 1) * LANES] for k in range(2)], axis=0)
        for t in range(buckets)
    ]
    for g in range(groups // 2):
        tile = packed[:, g * LANES : (g + 1) * LANES]
        turned = pltpu.roll(tile, bands, 1)
        pair = (jnp.where(low8, tile[:8], turned[8:]), jnp.where(low8, turned[:8], tile[8:]))
        for h in range(2):
            for t in range(slabs):
                block = (2 * g + h) * slabs + t
                send[block, 0:8, :] = first[t]
                send[block, 8:16, :] = jnp.where(last, fill[t].astype(F32), pair[h])


def joined(even, odd, low, bands):
    return jnp.concatenate(
        [jnp.where(low, even, pltpu.roll(odd, bands, 1)), jnp.where(low, pltpu.roll(even, bands, 1), odd)], axis=0
    )


def middle_kernel(groups, slabs, recv, partial, left, source_index, source_coeffs, source_vector, knots, own, *refs):
    later_in, refs, semaphores = refs[:4], refs[4:-1], refs[-1]
    buckets, capacity = left.shape
    source_dev = source_vector.shape[1]
    knot_dev = knots.shape[2]
    bands = knot_dev // KB
    shift = bands.bit_length() - 1
    capacity_shift = capacity.bit_length() - 1
    devices = groups * slabs
    packets = groups * bands
    alpha = own[16:17, 0:1]
    my_slab = lax.axis_index("tm")
    moved, (raw_out, gradient_source, gradient_knot, sums) = refs[: 2 * slabs], refs[2 * slabs : -4]
    later = fetch(later_in, refs[-4:], semaphores)
    low = iota((8, LANES), 1) < bands
    slot = iota((1, capacity), 1).astype(F32)

    indices, weighted = [], []
    squares = jnp.zeros((1, capacity), F32)
    cross = jnp.zeros((1, capacity), F32)
    for k in range(slabs):
        t = lax.rem(my_slab + (slabs - k), slabs)
        table = jnp.concatenate(
            [
                joined(recv[2 * g * slabs + t, 0:8, :], recv[(2 * g + 1) * slabs + t, 0:8, :], low, bands)
                for g in range(groups // 2)
            ],
            axis=1,
        )
        block = moved[2 * k][:, my_slab, :]
        coeffs = jnp.concatenate(
            [pad_rows(block[: ROWS // 2], 8), pad_rows(block[ROWS // 2 :], 8)], axis=0
        )
        found = pick(table, moved[2 * k + 1][pl.ds(my_slab, 1), :])
        image = jnp.sum(coeffs * found, axis=0, keepdims=True)
        raw = partial[pl.ds(t, 1), :] + jnp.where(slot < own[pl.ds(17 + t, 1), 0:1], image, 0.0)
        raw_out[pl.ds(t, 1), :] = raw
        squares = squares + raw * raw
        cross = cross + raw * (raw + alpha * left[pl.ds(t, 1), :])
        indices.append(source_index[pl.ds(t, 1), :])
        weighted.append(pad_rows(source_coeffs[:, t, :] * raw, 8))
    gathered_sum = put(jnp.concatenate(weighted, axis=1), jnp.concatenate(indices, axis=1), source_dev)
    gradient_source[...] = gathered_sum[:5]

    packet = jnp.concatenate(
        [
            joined(
                recv[2 * g * slabs + my_slab, 8:16, :], recv[(2 * g + 1) * slabs + my_slab, 8:16, :], low, bands
            )
            for g in range(groups // 2)
        ],
        axis=1,
    )
    band = packet[6:7].astype(I32)
    place = packet[14:15].astype(I32)
    inner = place & (capacity - 1)
    sender = (iota((1, packets), 1) >> shift) * slabs + (place >> capacity_shift)
    chosen = iota((devices, packets), 0) == sender
    partials = jnp.concatenate([recv[:, 6, :], recv[:, 7, :]], axis=1)
    found = pick(partials, inner)
    fills = jnp.concatenate([recv[:, 15, :]] * (packets // LANES), axis=1)
    partial_packet = jnp.sum(jnp.where(chosen, found, 0.0), axis=0, keepdims=True)
    fill_packet = jnp.sum(jnp.where(chosen, fills, 0.0), axis=0, keepdims=True)
    image = jnp.sum(packet * pick(own[0:16, 0:bands], band), axis=0, keepdims=True)
    raw = jnp.where(inner.astype(F32) < fill_packet, partial_packet + image, 0.0)
    collected = put(packet * raw, band, bands)
    hit = iota((bands, knot_dev), 0) == (iota((bands, knot_dev), 1) >> 2)
    spread = fold3(dot(split3(collected), jnp.where(hit, 1.0, 0.0).astype(BF16)))
    held, axis_of, offset = row_parts((16, knot_dev))
    spread = jnp.where(held & ((iota((16, knot_dev), 1) & (KB - 1)) == offset), spread, 0.0)
    knot_squares = jnp.zeros((1, knot_dev), F32)
    knot_old = jnp.zeros((1, knot_dev), F32)
    for a in range(3):
        total = jnp.sum(jnp.where(axis_of == a, spread, 0.0), axis=0, keepdims=True)
        gradient_knot[a] = total
        knot_squares = knot_squares + total * total
        knot_old = knot_old + knots[a] * knots[a]

    own_squares = jnp.sum(squares)
    cross_sum = jnp.sum(cross)
    gradient_squares = jnp.sum(gathered_sum * gathered_sum) + jnp.sum(knot_squares)
    old = source_vector[...]
    old_squares = jnp.sum(old * old) + jnp.sum(knot_old)
    lane = iota((devices, LANES), 1)
    sums[...] = jnp.where(
        lane == 0,
        own_squares,
        jnp.where(lane == 1, gradient_squares, jnp.where(lane == 2, cross_sum, old_squares)),
    )
    for copy in later:
        copy.wait()


def after_kernel(total_obs, unknowns, sums, own, raw, gradient_source, gradient_knot, source_vector, knots, source_search, knot_search, source_solution, knot_solution, left_next, source_next, knot_next, search_source, search_knot, solution_source, solution_knot, recurrence_next):
    ratio = unknowns / total_obs
    pivot, remainder = own[16:17, 1:2], own[16:17, 2:3]
    total = jnp.sum(sums[...], axis=0, keepdims=True)
    s0, s1, s2, s3 = (total[:, k : k + 1] for k in range(4))
    beta = jnp.sqrt(s0 / total_obs + EPSILON)
    scaled = ratio / beta
    alpha_square = scaled * scaled * s1 - 2.0 * ratio * s2 + beta * beta * s3
    alpha_next = jnp.sqrt(alpha_square / unknowns + EPSILON)
    radius = jnp.sqrt(pivot * pivot + beta * beta)
    cosine = pivot / radius
    sine = beta / radius
    gain = cosine * remainder / radius
    turn = sine * alpha_next / radius
    one_gradient = scaled / alpha_next
    one_vector = beta / alpha_next
    left_next[...] = raw[...] / beta
    search = source_search[...]
    value = one_gradient * gradient_source[...] - one_vector * source_vector[...]
    source_next[...] = value
    search_source[...] = value - turn * search
    solution_source[...] = source_solution[...] + gain * search
    for a in range(3):
        search = knot_search[a]
        value = one_gradient * gradient_knot[a] - one_vector * knots[a]
        knot_next[a] = value
        search_knot[a] = value - turn * search
        solution_knot[a] = knot_solution[a] + gain * search
    for k, value in enumerate((alpha_next, beta, -cosine * alpha_next, sine * remainder)):
        recurrence_next[k] = value[0, 0]


VMEM = pl.BlockSpec(memory_space=pltpu.VMEM)
SMEM = pl.BlockSpec(memory_space=pltpu.SMEM)
HBM = pl.BlockSpec(memory_space=pltpu.HBM)


def shards(
    left_vector,
    source_coeffs,
    knot_coeffs,
    source_index,
    band_start,
    bucket_fill,
    source_vector,
    knot_vector,
    source_search,
    knot_search,
    source_solution,
    knot_solution,
    recurrence,
):
    slabs = lax.axis_size("tm")
    groups = lax.axis_size("src")
    devices = slabs * groups
    buckets, capacity = left_vector.shape
    source_dev = source_vector.shape[1]
    knot_dev = knot_vector.shape[2]
    total_obs = buckets * capacity * devices
    unknowns = (5 * source_dev + 3 * knot_dev) * devices
    params = pltpu.CompilerParams(vmem_limit_bytes=48 * 1024 * 1024)
    shape = jax.ShapeDtypeStruct

    moved = []
    for k in range(1, slabs):
        shifted = [(t, (t + k) % slabs) for t in range(slabs)]
        moved += [lax.ppermute(knot_coeffs, "tm", shifted), lax.ppermute(band_start, "tm", shifted)]

    fill = bucket_fill.reshape(-1)
    operands = (
        source_index,
        source_coeffs,
        source_vector,
        left_vector,
        fill,
        recurrence,
        knot_coeffs,
        band_start,
        knot_vector,
    )
    send, partial, own = pl.pallas_call(
        functools.partial(before_kernel, groups, slabs),
        out_shape=(
            pltpu.VMEM((devices, 16, LANES), F32),
            shape((buckets, capacity), F32),
            shape((16 + 8 * pl.cdiv(1 + buckets, 8), LANES), F32),
        ),
        in_specs=[HBM] * len(operands),
        out_specs=(VMEM, VMEM, VMEM),
        scratch_shapes=[(pltpu.SMEM if x.ndim == 1 else pltpu.VMEM)(x.shape, x.dtype) for x in operands]
        + [pltpu.SemaphoreType.DMA((len(operands),))],
        compiler_params=params,
        name="before",
    )(*(pltpu.with_memory_space_constraint(x, pltpu.HBM) for x in operands))
    recv = lax.all_to_all(send, ("src", "tm"), split_axis=0, concat_axis=0, tiled=True)
    later = (source_search, knot_search, source_solution, knot_solution)
    raw, gradient_source, gradient_knot, sums, *later = pl.pallas_call(
        functools.partial(middle_kernel, groups, slabs),
        out_shape=(
            shape((buckets, capacity), F32),
            shape((5, source_dev), F32),
            shape((3, 1, knot_dev), F32),
            shape((devices, LANES), F32),
            *(shape(x.shape, F32) for x in later),
        ),
        in_specs=[VMEM] * 8 + [HBM] * 4 + [VMEM] * (2 * slabs),
        out_specs=(VMEM,) * 8,
        scratch_shapes=[pltpu.SemaphoreType.DMA((4,))],
        compiler_params=params,
        name="middle",
    )(
        recv,
        partial,
        left_vector,
        source_index,
        source_coeffs,
        source_vector,
        knot_vector,
        own,
        *later,
        knot_coeffs,
        band_start,
        *moved,
    )
    sums = lax.all_to_all(sums, ("src", "tm"), split_axis=0, concat_axis=0, tiled=True)
    like = [shape(x.shape, F32) for x in (left_vector, source_vector, knot_vector)]
    outs = pl.pallas_call(
        functools.partial(after_kernel, total_obs, unknowns),
        out_shape=(like[0], like[1], like[2], like[1], like[2], like[1], like[2], shape((4,), F32)),
        in_specs=[VMEM] * 11,
        out_specs=(VMEM,) * 7 + (SMEM,),
        compiler_params=params,
        name="after",
    )(
        sums,
        own,
        raw,
        gradient_source,
        gradient_knot,
        source_vector,
        knot_vector,
        *later,
    )
    return outs


def solution(mesh):
    wide = ("src", "tm")
    flat = P(None, wide)
    knot = P(None, "tm", "src")
    in_specs = (flat, P(None, None, wide), P(None, None, wide), flat, flat, flat, flat, knot, flat, knot, flat, knot, P())
    out_specs = (flat, flat, knot, flat, knot, flat, knot, P())
    return jax.shard_map(shards, mesh=mesh, in_specs=in_specs, out_specs=out_specs, check_vma=False)
```

```python
import functools

import jax
import jax.numpy as jnp
from jax import lax
from jax.experimental import pallas as pl
from jax.experimental.pallas import tpu as pltpu
from jax.sharding import PartitionSpec as P

KB = 4
ROWS = 3 * KB
BLOCK = 14
LANES = 128
EPSILON = 1e-06
F32 = jnp.float32
BF16 = jnp.bfloat16
I32 = jnp.int32


def iota(shape, axis):
    return lax.broadcasted_iota(I32, shape, axis)


def split3(x):
    hi = x.astype(BF16).astype(F32)
    rest = x - hi
    mid = rest.astype(BF16).astype(F32)
    return jnp.concatenate([hi, mid, rest - mid], axis=0).astype(BF16)


def fold3(y):
    n = y.shape[0] // 3
    return (y[2 * n :] + y[n : 2 * n]) + y[:n]


def dot(a, b):
    return lax.dot_general(a, b, (((1,), (0,)), ((), ())), preferred_element_type=F32)


def dot_nt(a, b):
    return lax.dot_general(a, b, (((1,), (1,)), ((), ())), preferred_element_type=F32)


WIDE = 256


def pick(values, index):
    rows, count = values.shape
    width = min(count, WIDE)
    parts = count // width
    stacked = jnp.concatenate([values[:, h * width : (h + 1) * width] for h in range(parts)], axis=0)
    found = fold3(dot(split3(stacked), onehot(width, index & (width - 1))))
    high = index >> (width.bit_length() - 1)
    result = found[:rows]
    for h in range(1, parts):
        result = jnp.where(high == h, found[h * rows : (h + 1) * rows], result)
    return result


def put(values, index, count):
    rows = values.shape[0]
    width = min(count, WIDE)
    parts = count // width
    high = index >> (width.bit_length() - 1)
    if parts > 1:
        values = jnp.concatenate([jnp.where(high == h, values, 0.0) for h in range(parts)], axis=0)
    sums = fold3(dot_nt(split3(values), onehot(width, index & (width - 1))))
    return jnp.concatenate([sums[h * rows : (h + 1) * rows] for h in range(parts)], axis=1)


def onehot(count, index):
    hit = iota((count, index.shape[1]), 0) == index
    return jnp.where(hit, 1.0, 0.0).astype(BF16)


def pad_rows(x, n):
    return jnp.concatenate([x, jnp.zeros((n - x.shape[0], x.shape[1]), F32)], axis=0)


def row_parts(shape):
    row = iota(shape, 0)
    upper = (row >= 8).astype(I32)
    held = (row - 8 * upper) < ROWS // 2
    c = row - 2 * upper
    return held, c >> 2, c & (KB - 1)


def halves(x, low):
    return jnp.where(low, x[:8], x[8:])


def fetch(sources, targets, semaphores):
    copies = [pltpu.make_async_copy(a, b, semaphores.at[k]) for k, (a, b) in enumerate(zip(sources, targets))]
    for copy in copies:
        copy.start()
    return copies


def before_kernel(groups, slabs, *refs):
    sources, (send, partial_out, own), targets, semaphores = refs[:13], refs[13:16], refs[16:29], refs[29]
    order = [*range(7), 11, 12, *range(7, 11)]
    copies = fetch([sources[k] for k in order], [targets[k] for k in order], semaphores)
    for copy in copies[:9]:
        copy.wait()
    fill, recurrence, source_index, source_coeffs, source_vector, left, knot_coeffs, band, knots = (
        *targets[-2:],
        *targets[:7],
    )
    buckets, capacity = left.shape
    source_dev = source_vector.shape[1]
    knot_dev = knots.shape[2]
    bands = knot_dev // KB
    shift = bands.bit_length() - 1
    alpha = recurrence[0]
    low8 = iota((8, LANES), 1) < bands
    slot = iota((1, capacity), 1)

    index = jnp.concatenate([source_index[pl.ds(t, 1), :] for t in range(buckets)], axis=1)
    picked = pick(pad_rows(source_vector[...], 8), index)[:5]
    partial = []
    for t in range(buckets):
        image = jnp.sum(source_coeffs[:, t, :] * picked[:, t * capacity : (t + 1) * capacity], axis=0, keepdims=True)
        partial.append(jnp.where(slot < fill[t], image - alpha * left[pl.ds(t, 1), :], 0.0))
        partial_out[pl.ds(t, 1), :] = partial[t]

    my_slab = lax.axis_index("tm")
    total = jnp.zeros((groups, 1), F32)
    before = jnp.where(iota((capacity, capacity), 0) < iota((capacity, capacity), 1), 1.0, 0.0).astype(BF16)
    targets, columns = [], []
    for i in range(buckets):
        bands_i = band[pl.ds(i, 1), :]
        owner = bands_i >> shift
        named = jnp.where(iota((groups, capacity), 0) == owner, 1.0, 0.0)
        count = dot(named.astype(BF16), before) + total
        rank = jnp.sum(named * count, axis=0, keepdims=True).astype(I32)
        total = total + jnp.sum(named, axis=1, keepdims=True)
        targets.append(owner * bands + rank)
        local = (bands_i - owner * bands).astype(F32)
        place = (slot + i * capacity).astype(F32)
        zero = jnp.zeros((1, capacity), F32)
        here = my_slab == i
        coeffs = jnp.where(here & (slot >= fill[i]), 0.0, knot_coeffs[:, i, :])
        known = jnp.where(here, partial[i], 0.0)
        columns.append(
            jnp.concatenate([coeffs[: ROWS // 2], local, known, coeffs[ROWS // 2 :], place, zero], axis=0)
        )
    packed = put(jnp.concatenate(columns, axis=1), jnp.concatenate(targets, axis=1), groups * bands)

    held, axis_of, offset = row_parts((16, knot_dev))
    spread = jnp.zeros((16, knot_dev), F32)
    for a in range(3):
        spread = jnp.where(axis_of == a, knots[a], spread)
    spread = jnp.where(held & ((iota((16, knot_dev), 1) & (KB - 1)) == offset), spread, 0.0)
    hit = (iota((knot_dev, LANES), 0) >> 2) == (iota((knot_dev, LANES), 1) & (bands - 1))
    rows = fold3(dot(split3(spread), jnp.where(hit, 1.0, 0.0).astype(BF16)))
    own[0:16, :] = rows
    row, lane = iota((own.shape[0] - 16, LANES), 0), iota((own.shape[0] - 16, LANES), 1)
    scalars = jnp.where(lane == 0, alpha, jnp.where(lane == 1, recurrence[1], recurrence[2]))
    for t in range(buckets):
        scalars = jnp.where(row == 1 + t, fill[t].astype(F32), scalars)
    own[16:, :] = scalars
    knot_rows = halves(rows, low8)[: ROWS // 2]

    other = [
        jnp.concatenate(
            [partial[t][:, k * LANES : (k + 1) * LANES] for k in range(capacity // LANES)]
            + [jnp.full((8 - capacity // LANES, LANES), fill[t].astype(F32))],
            axis=0,
        )
        for t in range(buckets)
    ]
    for g in range(groups // 2):
        tile = packed[:, g * LANES : (g + 1) * LANES]
        turned = pltpu.roll(tile, bands, 1)
        pair = (jnp.where(low8, tile[:8], turned[8:]), jnp.where(low8, turned[:8], tile[8:]))
        for h in range(2):
            for t in range(slabs):
                row = ((2 * g + h) * slabs + t) * BLOCK
                send[row : row + 8, :] = jnp.where(my_slab == t, pair[h], other[t])
                send[row + 8 : row + BLOCK, :] = knot_rows
    for copy in copies[9:]:
        copy.wait()


def joined(even, odd, low, bands):
    return jnp.concatenate(
        [jnp.where(low, even, pltpu.roll(odd, bands, 1)), jnp.where(low, pltpu.roll(even, bands, 1), odd)], axis=0
    )


def middle_kernel(groups, slabs, recv, partial, left, source_index, source_coeffs, source_vector, knots, own, *refs):
    buckets, capacity = left.shape
    source_dev = source_vector.shape[1]
    knot_dev = knots.shape[2]
    bands = knot_dev // KB
    shift = bands.bit_length() - 1
    capacity_shift = capacity.bit_length() - 1
    devices = groups * slabs
    packets = groups * bands
    alpha = own[16:17, 0:1]
    my_slab = lax.axis_index("tm")
    moved, (raw_out, gradient_source, gradient_knot, sums) = refs[: 2 * slabs], refs[2 * slabs :]
    low = iota((8, LANES), 1) < bands
    slot = iota((1, capacity), 1).astype(F32)

    indices, weighted = [], []
    squares = jnp.zeros((1, capacity), F32)
    cross = jnp.zeros((1, capacity), F32)
    def blocks(t, start):
        rows = [((2 * g + h) * slabs + t) * BLOCK + start for g in range(groups // 2) for h in range(2)]
        loaded = [recv[row : row + 8, :] for row in rows]
        return jnp.concatenate([joined(*loaded[k : k + 2], low, bands) for k in range(0, groups, 2)], axis=1)

    def of_slab(t, values):
        result = values[0]
        for k in range(1, slabs):
            result = jnp.where(my_slab == (t + k) % slabs, values[k], result)
        return result

    coeffs_of = [moved[2 * k][:, my_slab, :] for k in range(slabs)]
    bands_of = [moved[2 * k + 1][pl.ds(my_slab, 1), :] for k in range(slabs)]
    gap = jnp.zeros((2, capacity), F32)
    for t in range(slabs):
        block = of_slab(t, coeffs_of)
        coeffs = jnp.concatenate([gap, block[: ROWS // 2], gap, block[ROWS // 2 :]], axis=0)
        found = pick(blocks(t, 6), of_slab(t, bands_of))
        image = jnp.sum(coeffs * found, axis=0, keepdims=True)
        raw = partial[pl.ds(t, 1), :] + jnp.where(slot < own[pl.ds(17 + t, 1), 0:1], image, 0.0)
        raw_out[pl.ds(t, 1), :] = raw
        squares = squares + raw * raw
        cross = cross + raw * (raw + alpha * left[pl.ds(t, 1), :])
        indices.append(source_index[pl.ds(t, 1), :])
        weighted.append(pad_rows(source_coeffs[:, t, :] * raw, 8))
    gathered_sum = put(jnp.concatenate(weighted, axis=1), jnp.concatenate(indices, axis=1), source_dev)
    gradient_source[...] = gathered_sum[:5]

    packet = blocks(0, 0)
    for t in range(1, slabs):
        packet = jnp.where(my_slab == t, blocks(t, 0), packet)
    band = packet[6:7].astype(I32)
    place = packet[14:15].astype(I32)
    inner = place & (capacity - 1)
    first = place >> capacity_shift
    senders = WIDE // bands
    member = senders * slabs
    part = [recv[pl.ds(k, devices, stride=BLOCK), :] for k in range(capacity // LANES + 1)]
    partials = jnp.concatenate(part[:-1], axis=1)
    fills = jnp.concatenate([part[-1]] * (WIDE // LANES), axis=1)
    row = iota((member, WIDE), 0)
    sender = (iota((1, WIDE), 1) >> shift) * slabs
    found = []
    for q in range(packets // WIDE):
        lanes = slice(q * WIDE, (q + 1) * WIDE)
        rows = slice(q * member, (q + 1) * member)
        chosen = row == sender + first[:, lanes]
        values = pick(partials[rows], inner[:, lanes])
        valid = jnp.sum(jnp.where(chosen, fills[rows], 0.0), axis=0, keepdims=True)
        found.append((jnp.sum(jnp.where(chosen, values, 0.0), axis=0, keepdims=True), valid))
    partial_packet, fill_packet = (jnp.concatenate(x, axis=1) for x in zip(*found))
    image = jnp.sum(packet * pick(own[0:16, 0:bands], band), axis=0, keepdims=True)
    known = first == my_slab
    partial_packet = jnp.where(known, packet[7:8], partial_packet)
    raw = jnp.where(known | (inner.astype(F32) < fill_packet), partial_packet + image, 0.0)
    hit = (iota((knot_dev, packets), 0) >> 2) == band
    spread = fold3(dot_nt(split3(packet * raw), jnp.where(hit, 1.0, 0.0).astype(BF16)))
    held, axis_of, offset = row_parts((16, knot_dev))
    spread = jnp.where(held & ((iota((16, knot_dev), 1) & (KB - 1)) == offset), spread, 0.0)
    for a in range(3):
        gradient_knot[a] = jnp.sum(jnp.where(axis_of == a, spread, 0.0), axis=0, keepdims=True)

    def across(x):
        x = jnp.sum(x, axis=0, keepdims=True)
        return functools.reduce(jnp.add, [x[:, k : k + LANES] for k in range(0, x.shape[1], LANES)])

    old = source_vector[...]
    old_knots = sum(knots[a] * knots[a] for a in range(3))
    new_knots = sum(gradient_knot[a] * gradient_knot[a] for a in range(3))
    parts = (
        across(squares),
        across(gathered_sum * gathered_sum) + across(new_knots),
        across(cross),
        across(old * old) + across(old_knots),
    )
    quarter = iota((8, LANES), 0)
    stacked = jnp.zeros((8, LANES), F32)
    for k, part in enumerate(parts):
        stacked = jnp.where(quarter == k, part, stacked)
    totals = jnp.where(quarter == iota((8, LANES), 1), jnp.sum(stacked, axis=1, keepdims=True), 0.0)
    sums[...] = jnp.broadcast_to(jnp.sum(totals, axis=0, keepdims=True), sums.shape)


def after_kernel(total_obs, unknowns, sums, own, raw, gradient_source, gradient_knot, source_vector, knots, source_search, knot_search, source_solution, knot_solution, left_next, source_next, knot_next, search_source, search_knot, solution_source, solution_knot, recurrence_next):
    ratio = unknowns / total_obs
    pivot, remainder = own[16:17, 1:2], own[16:17, 2:3]
    total = jnp.sum(sums[...], axis=0, keepdims=True)
    s0, s1, s2, s3 = (total[:, k : k + 1] for k in range(4))
    beta = jnp.sqrt(s0 / total_obs + EPSILON)
    scaled = ratio / beta
    alpha_square = scaled * scaled * s1 - 2.0 * ratio * s2 + beta * beta * s3
    alpha_next = jnp.sqrt(alpha_square / unknowns + EPSILON)
    radius = jnp.sqrt(pivot * pivot + beta * beta)
    cosine = pivot / radius
    sine = beta / radius
    gain = cosine * remainder / radius
    turn = sine * alpha_next / radius
    one_gradient = scaled / alpha_next
    one_vector = beta / alpha_next
    left_next[...] = raw[...] / beta
    search = source_search[...]
    value = one_gradient * gradient_source[...] - one_vector * source_vector[...]
    source_next[...] = value
    search_source[...] = value - turn * search
    solution_source[...] = source_solution[...] + gain * search
    for a in range(3):
        search = knot_search[a]
        value = one_gradient * gradient_knot[a] - one_vector * knots[a]
        knot_next[a] = value
        search_knot[a] = value - turn * search
        solution_knot[a] = knot_solution[a] + gain * search
    for k, value in enumerate((alpha_next, beta, -cosine * alpha_next, sine * remainder)):
        recurrence_next[k] = value[0, 0]


VMEM = pl.BlockSpec(memory_space=pltpu.VMEM)
SMEM = pl.BlockSpec(memory_space=pltpu.SMEM)
HBM = pl.BlockSpec(memory_space=pltpu.HBM)


def shards(
    left_vector,
    source_coeffs,
    knot_coeffs,
    source_index,
    band_start,
    bucket_fill,
    source_vector,
    knot_vector,
    source_search,
    knot_search,
    source_solution,
    knot_solution,
    recurrence,
):
    slabs = lax.axis_size("tm")
    groups = lax.axis_size("src")
    devices = slabs * groups
    buckets, capacity = left_vector.shape
    source_dev = source_vector.shape[1]
    knot_dev = knot_vector.shape[2]
    total_obs = buckets * capacity * devices
    unknowns = (5 * source_dev + 3 * knot_dev) * devices
    params = pltpu.CompilerParams(vmem_limit_bytes=48 * 1024 * 1024)
    shape = jax.ShapeDtypeStruct

    fill = bucket_fill.reshape(-1)
    operands = (
        source_index,
        source_coeffs,
        source_vector,
        left_vector,
        knot_coeffs,
        band_start,
        knot_vector,
        source_search,
        knot_search,
        source_solution,
        knot_solution,
        fill,
        recurrence,
    )
    send, partial, own, *held = pl.pallas_call(
        functools.partial(before_kernel, groups, slabs),
        out_shape=(
            shape((devices * BLOCK, LANES), F32),
            shape((buckets, capacity), F32),
            shape((16 + 8 * pl.cdiv(1 + buckets, 8), LANES), F32),
            *(pltpu.VMEM(x.shape, x.dtype) for x in operands[:-2]),
        ),
        in_specs=[HBM] * len(operands),
        out_specs=(VMEM,) * 14,
        scratch_shapes=[pltpu.SMEM(x.shape, x.dtype) for x in operands[-2:]]
        + [pltpu.SemaphoreType.DMA((len(operands),))],
        compiler_params=params,
        name="before",
    )(*(pltpu.with_memory_space_constraint(x, pltpu.HBM) for x in operands))
    source_index, source_coeffs, source_vector, left_held, knot_coeffs, band_start, knots_held, *later = held
    moved = []
    for k in range(1, slabs):
        shifted = [(t, (t + k) % slabs) for t in range(slabs)]
        moved += [lax.ppermute(knot_coeffs, "tm", shifted), lax.ppermute(band_start, "tm", shifted)]

    send = send.reshape(devices * BLOCK, 1, LANES)
    recv = lax.all_to_all(send, ("src", "tm"), split_axis=0, concat_axis=0, tiled=True)
    recv = recv.reshape(devices * BLOCK, LANES)
    raw, gradient_source, gradient_knot, sums = pl.pallas_call(
        functools.partial(middle_kernel, groups, slabs),
        out_shape=(
            shape((buckets, capacity), F32),
            shape((5, source_dev), F32),
            shape((3, 1, knot_dev), F32),
            shape((devices, LANES), F32),
        ),
        in_specs=[VMEM] * (8 + 2 * slabs),
        out_specs=(VMEM,) * 4,
        compiler_params=params,
        name="middle",
    )(
        recv,
        partial,
        left_held,
        source_index,
        source_coeffs,
        source_vector,
        knots_held,
        own,
        knot_coeffs,
        band_start,
        *moved,
    )
    sums = lax.all_to_all(sums, ("src", "tm"), split_axis=0, concat_axis=0, tiled=True)
    like = [shape(x.shape, F32) for x in (left_vector, source_vector, knot_vector)]
    outs = pl.pallas_call(
        functools.partial(after_kernel, total_obs, unknowns),
        out_shape=(like[0], like[1], like[2], like[1], like[2], like[1], like[2], shape((4,), F32)),
        in_specs=[VMEM] * 11,
        out_specs=(VMEM,) * 7 + (SMEM,),
        compiler_params=params,
        name="after",
    )(
        sums,
        own,
        raw,
        gradient_source,
        gradient_knot,
        source_vector,
        knots_held,
        *later,
    )
    return outs


def solution(mesh):
    wide = ("src", "tm")
    flat = P(None, wide)
    knot = P(None, "tm", "src")
    in_specs = (flat, P(None, None, wide), P(None, None, wide), flat, flat, flat, flat, knot, flat, knot, flat, knot, P())
    out_specs = (flat, flat, knot, flat, knot, flat, knot, P())
    return jax.shard_map(shards, mesh=mesh, in_specs=in_specs, out_specs=out_specs, check_vma=False)
```

```python
import functools

import jax
import jax.numpy as jnp
from jax import lax
from jax.experimental import pallas as pl
from jax.experimental.pallas import tpu as pltpu
from jax.sharding import PartitionSpec as P

KB = 4
ROWS = 3 * KB
BLOCK = 14
LANES = 128
EPSILON = 1e-06
F32 = jnp.float32
BF16 = jnp.bfloat16
I32 = jnp.int32


def iota(shape, axis):
    return lax.broadcasted_iota(I32, shape, axis)


def thirds(x):
    hi = x.astype(BF16).astype(F32)
    rest = x - hi
    mid = rest.astype(BF16).astype(F32)
    return jnp.concatenate([hi, mid, rest - mid], axis=0)


def split3(x):
    return thirds(x).astype(BF16)


def fold3(y):
    n = y.shape[0] // 3
    return (y[2 * n :] + y[n : 2 * n]) + y[:n]


def dot(a, b):
    return lax.dot_general(a, b, (((1,), (0,)), ((), ())), preferred_element_type=F32)


def dot_nt(a, b):
    return lax.dot_general(a, b, (((1,), (1,)), ((), ())), preferred_element_type=F32)


WIDE = 256


def pick(values, index):
    rows, count = values.shape
    width = min(count, WIDE)
    parts = count // width
    stacked = jnp.concatenate([values[:, h * width : (h + 1) * width] for h in range(parts)], axis=0)
    found = fold3(dot(split3(stacked), onehot(width, index & (width - 1))))
    high = index >> (width.bit_length() - 1)
    result = found[:rows]
    for h in range(1, parts):
        result = jnp.where(high == h, found[h * rows : (h + 1) * rows], result)
    return result


def put(values, index, count):
    rows = 3 * values.shape[0]
    width = min(count, WIDE)
    parts = count // width
    high = index >> (width.bit_length() - 1)
    values = thirds(values)
    if parts > 1:
        values = jnp.concatenate([jnp.where(high == h, values, 0.0) for h in range(parts)], axis=0)
    sums = dot_nt(values.astype(BF16), onehot(width, index & (width - 1)))
    return jnp.concatenate([fold3(sums[h * rows : (h + 1) * rows]) for h in range(parts)], axis=1)


def onehot(count, index):
    hit = iota((count, index.shape[1]), 0) == index
    return jnp.where(hit, 1.0, 0.0).astype(BF16)


def pad_rows(x, n):
    return jnp.concatenate([x, jnp.zeros((n - x.shape[0], x.shape[1]), F32)], axis=0)


def row_parts(shape):
    row = iota(shape, 0)
    upper = (row >= 8).astype(I32)
    held = (row - 8 * upper) < ROWS // 2
    c = row - 2 * upper
    return held, c >> 2, c & (KB - 1)


def halves(x, low):
    return jnp.where(low, x[:8], x[8:])


def fetch(sources, targets, semaphores):
    copies = [pltpu.make_async_copy(a, b, semaphores.at[k]) for k, (a, b) in enumerate(zip(sources, targets))]
    for copy in copies:
        copy.start()
    return copies


def before_kernel(groups, slabs, *refs):
    sources, (send, partial_out, own), targets, semaphores = refs[:13], refs[13:16], refs[16:29], refs[29]
    order = [*range(7), 11, 12, *range(7, 11)]
    copies = fetch([sources[k] for k in order], [targets[k] for k in order], semaphores)
    for copy in copies[:9]:
        copy.wait()
    fill, recurrence, source_index, source_coeffs, source_vector, left, knot_coeffs, band, knots = (
        *targets[-2:],
        *targets[:7],
    )
    buckets, capacity = left.shape
    source_dev = source_vector.shape[1]
    knot_dev = knots.shape[2]
    bands = knot_dev // KB
    shift = bands.bit_length() - 1
    alpha = recurrence[0]
    low8 = iota((8, LANES), 1) < bands
    slot = iota((1, capacity), 1)

    my_slab = lax.axis_index("tm")
    total = jnp.zeros((groups, 1), F32)
    before = jnp.where(iota((capacity, capacity), 0) < iota((capacity, capacity), 1), 1.0, 0.0).astype(BF16)
    targets, columns = [], []
    for i in range(buckets):
        bands_i = band[pl.ds(i, 1), :]
        owner = bands_i >> shift
        named = jnp.where(iota((groups, capacity), 0) == owner, 1.0, 0.0)
        count = dot(named.astype(BF16), before) + total
        rank = jnp.sum(named * count, axis=0, keepdims=True).astype(I32)
        total = total + jnp.sum(named, axis=1, keepdims=True)
        targets.append(owner * bands + rank)
    index = jnp.concatenate([source_index[pl.ds(t, 1), :] for t in range(buckets)], axis=1)
    picked = pick(pad_rows(source_vector[...], 8), index)[:5]
    partial = []
    for t in range(buckets):
        image = jnp.sum(source_coeffs[:, t, :] * picked[:, t * capacity : (t + 1) * capacity], axis=0, keepdims=True)
        partial.append(jnp.where(slot < fill[t], image - alpha * left[pl.ds(t, 1), :], 0.0))
        partial_out[pl.ds(t, 1), :] = partial[t]

    zero = jnp.zeros((1, capacity), F32)
    for i in range(buckets):
        local = (band[pl.ds(i, 1), :] & (bands - 1)).astype(F32)
        place = (slot + i * capacity).astype(F32)
        here = my_slab == i
        coeffs = jnp.where(here & (slot >= fill[i]), 0.0, knot_coeffs[:, i, :])
        known = jnp.where(here, partial[i], 0.0)
        columns.append(
            jnp.concatenate([coeffs[: ROWS // 2], local, known, coeffs[ROWS // 2 :], place, zero], axis=0)
        )
    packed = put(jnp.concatenate(columns, axis=1), jnp.concatenate(targets, axis=1), groups * bands)

    held, axis_of, offset = row_parts((16, knot_dev))
    spread = jnp.zeros((16, knot_dev), F32)
    for a in range(3):
        spread = jnp.where(axis_of == a, knots[a], spread)
    spread = jnp.where(held & ((iota((16, knot_dev), 1) & (KB - 1)) == offset), spread, 0.0)
    hit = (iota((knot_dev, LANES), 0) >> 2) == (iota((knot_dev, LANES), 1) & (bands - 1))
    rows = fold3(dot(split3(spread), jnp.where(hit, 1.0, 0.0).astype(BF16)))
    own[0:16, :] = rows
    row, lane = iota((own.shape[0] - 16, LANES), 0), iota((own.shape[0] - 16, LANES), 1)
    scalars = jnp.where(lane == 0, alpha, jnp.where(lane == 1, recurrence[1], recurrence[2]))
    for t in range(buckets):
        scalars = jnp.where(row == 1 + t, fill[t].astype(F32), scalars)
    own[16:, :] = scalars
    knot_rows = halves(rows, low8)[: ROWS // 2]

    other = [
        jnp.concatenate(
            [partial[t][:, k * LANES : (k + 1) * LANES] for k in range(capacity // LANES)]
            + [jnp.full((8 - capacity // LANES, LANES), fill[t].astype(F32))],
            axis=0,
        )
        for t in range(buckets)
    ]
    for g in range(groups // 2):
        tile = packed[:, g * LANES : (g + 1) * LANES]
        turned = pltpu.roll(tile, bands, 1)
        pair = (jnp.where(low8, tile[:8], turned[8:]), jnp.where(low8, turned[:8], tile[8:]))
        for h in range(2):
            for t in range(slabs):
                row = ((2 * g + h) * slabs + t) * BLOCK
                send[row : row + 8, :] = jnp.where(my_slab == t, pair[h], other[t])
                send[row + 8 : row + BLOCK, :] = knot_rows
    for copy in copies[9:]:
        copy.wait()


def joined(even, odd, low, bands):
    return jnp.concatenate(
        [jnp.where(low, even, pltpu.roll(odd, bands, 1)), jnp.where(low, pltpu.roll(even, bands, 1), odd)], axis=0
    )


def middle_kernel(groups, slabs, recv, partial, left, source_index, source_coeffs, source_vector, knots, own, *refs):
    buckets, capacity = left.shape
    source_dev = source_vector.shape[1]
    knot_dev = knots.shape[2]
    bands = knot_dev // KB
    shift = bands.bit_length() - 1
    capacity_shift = capacity.bit_length() - 1
    devices = groups * slabs
    packets = groups * bands
    alpha = own[16:17, 0:1]
    my_slab = lax.axis_index("tm")
    moved, (raw_out, gradient_source, gradient_knot, sums) = refs[: 2 * slabs], refs[2 * slabs :]
    low = iota((8, LANES), 1) < bands
    slot = iota((1, capacity), 1).astype(F32)

    def blocks(t, start):
        rows = [((2 * g + h) * slabs + t) * BLOCK + start for g in range(groups // 2) for h in range(2)]
        loaded = [recv[row : row + 8, :] for row in rows]
        return jnp.concatenate([joined(*loaded[k : k + 2], low, bands) for k in range(0, groups, 2)], axis=1)

    def of_slab(t, values):
        result = values[0]
        for k in range(1, slabs):
            result = jnp.where(my_slab == (t + k) % slabs, values[k], result)
        return result


    indices, weighted = [], []
    squares = jnp.zeros((1, capacity), F32)
    cross = jnp.zeros((1, capacity), F32)
    coeffs_of = [moved[2 * k][:, my_slab, :] for k in range(slabs)]
    bands_of = [moved[2 * k + 1][pl.ds(my_slab, 1), :] for k in range(slabs)]
    gap = jnp.zeros((2, capacity), F32)
    for t in range(slabs):
        block = of_slab(t, coeffs_of)
        coeffs = jnp.concatenate([gap, block[: ROWS // 2], gap, block[ROWS // 2 :]], axis=0)
        found = pick(blocks(t, 6), of_slab(t, bands_of))
        image = jnp.sum(coeffs * found, axis=0, keepdims=True)
        raw = partial[pl.ds(t, 1), :] + jnp.where(slot < own[pl.ds(17 + t, 1), 0:1], image, 0.0)
        raw_out[pl.ds(t, 1), :] = raw
        squares = squares + raw * raw
        cross = cross + raw * (raw + alpha * left[pl.ds(t, 1), :])
        indices.append(source_index[pl.ds(t, 1), :])
        weighted.append(pad_rows(source_coeffs[:, t, :] * raw, 8))
    packet = blocks(0, 0)
    for t in range(1, slabs):
        packet = jnp.where(my_slab == t, blocks(t, 0), packet)
    band = packet[6:7].astype(I32)
    place = packet[14:15].astype(I32)
    inner = place & (capacity - 1)
    first = place >> capacity_shift
    senders = WIDE // bands
    member = senders * slabs
    part = [recv[pl.ds(k, devices, stride=BLOCK), :] for k in range(capacity // LANES + 1)]
    partials = jnp.concatenate(part[:-1], axis=1)
    fills = jnp.concatenate([part[-1]] * (WIDE // LANES), axis=1)
    row = iota((member, WIDE), 0)
    sender = (iota((1, WIDE), 1) >> shift) * slabs
    found = []
    for q in range(packets // WIDE):
        lanes = slice(q * WIDE, (q + 1) * WIDE)
        rows = slice(q * member, (q + 1) * member)
        chosen = row == sender + first[:, lanes]
        values = pick(partials[rows], inner[:, lanes])
        valid = jnp.sum(jnp.where(chosen, fills[rows], 0.0), axis=0, keepdims=True)
        found.append((jnp.sum(jnp.where(chosen, values, 0.0), axis=0, keepdims=True), valid))
    partial_packet, fill_packet = (jnp.concatenate(x, axis=1) for x in zip(*found))
    image = jnp.sum(packet * pick(own[0:16, 0:bands], band), axis=0, keepdims=True)
    known = first == my_slab
    partial_packet = jnp.where(known, packet[7:8], partial_packet)
    packet_raw = jnp.where(known | (inner.astype(F32) < fill_packet), partial_packet + image, 0.0)
    hit = (iota((knot_dev, packets), 0) >> 2) == band
    spread = fold3(dot_nt(split3(packet * packet_raw), jnp.where(hit, 1.0, 0.0).astype(BF16)))
    held, axis_of, offset = row_parts((16, knot_dev))
    spread = jnp.where(held & ((iota((16, knot_dev), 1) & (KB - 1)) == offset), spread, 0.0)
    for a in range(3):
        gradient_knot[a] = jnp.sum(jnp.where(axis_of == a, spread, 0.0), axis=0, keepdims=True)

    gathered_sum = put(jnp.concatenate(weighted, axis=1), jnp.concatenate(indices, axis=1), source_dev)
    gradient_source[...] = gathered_sum[:5]
    def across(x):
        x = jnp.sum(x, axis=0, keepdims=True)
        return functools.reduce(jnp.add, [x[:, k : k + LANES] for k in range(0, x.shape[1], LANES)])

    old = source_vector[...]
    old_knots = sum(knots[a] * knots[a] for a in range(3))
    new_knots = sum(gradient_knot[a] * gradient_knot[a] for a in range(3))
    parts = (
        across(squares),
        across(gathered_sum * gathered_sum) + across(new_knots),
        across(cross),
        across(old * old) + across(old_knots),
    )
    quarter = iota((8, LANES), 0)
    stacked = jnp.zeros((8, LANES), F32)
    for k, part in enumerate(parts):
        stacked = jnp.where(quarter == k, part, stacked)
    totals = jnp.where(quarter == iota((8, LANES), 1), jnp.sum(stacked, axis=1, keepdims=True), 0.0)
    sums[...] = jnp.broadcast_to(jnp.sum(totals, axis=0, keepdims=True), sums.shape)


def after_kernel(total_obs, unknowns, sums, own, raw, gradient_source, gradient_knot, source_vector, knots, source_search, knot_search, source_solution, knot_solution, left_next, source_next, knot_next, search_source, search_knot, solution_source, solution_knot, recurrence_next):
    ratio = unknowns / total_obs
    pivot, remainder = own[16:17, 1:2], own[16:17, 2:3]
    total = jnp.sum(sums[...], axis=0, keepdims=True)
    s0, s1, s2, s3 = (total[:, k : k + 1] for k in range(4))
    beta = jnp.sqrt(s0 / total_obs + EPSILON)
    scaled = ratio / beta
    alpha_square = scaled * scaled * s1 - 2.0 * ratio * s2 + beta * beta * s3
    alpha_next = jnp.sqrt(alpha_square / unknowns + EPSILON)
    radius = jnp.sqrt(pivot * pivot + beta * beta)
    cosine = pivot / radius
    sine = beta / radius
    gain = cosine * remainder / radius
    turn = sine * alpha_next / radius
    one_gradient = scaled / alpha_next
    one_vector = beta / alpha_next
    left_next[...] = raw[...] / beta
    search = source_search[...]
    value = one_gradient * gradient_source[...] - one_vector * source_vector[...]
    source_next[...] = value
    search_source[...] = value - turn * search
    solution_source[...] = source_solution[...] + gain * search
    for a in range(3):
        search = knot_search[a]
        value = one_gradient * gradient_knot[a] - one_vector * knots[a]
        knot_next[a] = value
        search_knot[a] = value - turn * search
        solution_knot[a] = knot_solution[a] + gain * search
    for k, value in enumerate((alpha_next, beta, -cosine * alpha_next, sine * remainder)):
        recurrence_next[k] = value[0, 0]


VMEM = pl.BlockSpec(memory_space=pltpu.VMEM)
SMEM = pl.BlockSpec(memory_space=pltpu.SMEM)
HBM = pl.BlockSpec(memory_space=pltpu.HBM)


def shards(
    left_vector,
    source_coeffs,
    knot_coeffs,
    source_index,
    band_start,
    bucket_fill,
    source_vector,
    knot_vector,
    source_search,
    knot_search,
    source_solution,
    knot_solution,
    recurrence,
):
    slabs = lax.axis_size("tm")
    groups = lax.axis_size("src")
    devices = slabs * groups
    buckets, capacity = left_vector.shape
    source_dev = source_vector.shape[1]
    knot_dev = knot_vector.shape[2]
    total_obs = buckets * capacity * devices
    unknowns = (5 * source_dev + 3 * knot_dev) * devices
    params = pltpu.CompilerParams(vmem_limit_bytes=48 * 1024 * 1024)
    shape = jax.ShapeDtypeStruct

    fill = bucket_fill.reshape(-1)
    operands = (
        source_index,
        source_coeffs,
        source_vector,
        left_vector,
        knot_coeffs,
        band_start,
        knot_vector,
        source_search,
        knot_search,
        source_solution,
        knot_solution,
        fill,
        recurrence,
    )
    send, partial, own, *held = pl.pallas_call(
        functools.partial(before_kernel, groups, slabs),
        out_shape=(
            shape((devices * BLOCK, LANES), F32),
            shape((buckets, capacity), F32),
            shape((16 + 8 * pl.cdiv(1 + buckets, 8), LANES), F32),
            *(pltpu.VMEM(x.shape, x.dtype) for x in operands[:-2]),
        ),
        in_specs=[HBM] * len(operands),
        out_specs=(VMEM,) * 14,
        scratch_shapes=[pltpu.SMEM(x.shape, x.dtype) for x in operands[-2:]]
        + [pltpu.SemaphoreType.DMA((len(operands),))],
        compiler_params=params,
        name="before",
    )(*(pltpu.with_memory_space_constraint(x, pltpu.HBM) for x in operands))
    source_index, source_coeffs, source_vector, left_held, knot_coeffs, band_start, knots_held, *later = held
    moved = []
    for k in range(1, slabs):
        shifted = [(t, (t + k) % slabs) for t in range(slabs)]
        moved += [lax.ppermute(knot_coeffs, "tm", shifted), lax.ppermute(band_start, "tm", shifted)]

    send = send.reshape(devices * BLOCK, 1, LANES)
    recv = lax.all_to_all(send, ("src", "tm"), split_axis=0, concat_axis=0, tiled=True)
    recv = recv.reshape(devices * BLOCK, LANES)
    raw, gradient_source, gradient_knot, sums = pl.pallas_call(
        functools.partial(middle_kernel, groups, slabs),
        out_shape=(
            shape((buckets, capacity), F32),
            shape((5, source_dev), F32),
            shape((3, 1, knot_dev), F32),
            shape((devices, LANES), F32),
        ),
        in_specs=[VMEM] * (8 + 2 * slabs),
        out_specs=(VMEM,) * 4,
        compiler_params=params,
        name="middle",
    )(
        recv,
        partial,
        left_held,
        source_index,
        source_coeffs,
        source_vector,
        knots_held,
        own,
        knot_coeffs,
        band_start,
        *moved,
    )
    sums = lax.all_to_all(sums, ("src", "tm"), split_axis=0, concat_axis=0, tiled=True)
    like = [shape(x.shape, F32) for x in (left_vector, source_vector, knot_vector)]
    outs = pl.pallas_call(
        functools.partial(after_kernel, total_obs, unknowns),
        out_shape=(like[0], like[1], like[2], like[1], like[2], like[1], like[2], shape((4,), F32)),
        in_specs=[VMEM] * 11,
        out_specs=(VMEM,) * 7 + (SMEM,),
        compiler_params=params,
        name="after",
    )(
        sums,
        own,
        raw,
        gradient_source,
        gradient_knot,
        source_vector,
        knots_held,
        *later,
    )
    return outs


def solution(mesh):
    wide = ("src", "tm")
    flat = P(None, wide)
    knot = P(None, "tm", "src")
    in_specs = (flat, P(None, None, wide), P(None, None, wide), flat, flat, flat, flat, knot, flat, knot, flat, knot, P())
    out_specs = (flat, flat, knot, flat, knot, flat, knot, P())
    return jax.shard_map(shards, mesh=mesh, in_specs=in_specs, out_specs=out_specs, check_vma=False)
```

```python
import functools

import jax
import jax.numpy as jnp
from jax import lax
from jax.experimental import pallas as pl
from jax.experimental.pallas import tpu as pltpu
from jax.sharding import PartitionSpec as P

KB = 4
ROWS = 3 * KB
BLOCK = 14
LANES = 128
EPSILON = 1e-06
F32 = jnp.float32
BF16 = jnp.bfloat16
I32 = jnp.int32


def iota(shape, axis):
    return lax.broadcasted_iota(I32, shape, axis)


def thirds(x):
    hi = x.astype(BF16).astype(F32)
    rest = x - hi
    mid = rest.astype(BF16).astype(F32)
    return jnp.concatenate([hi, mid, rest - mid], axis=0)


def split3(x):
    return thirds(x).astype(BF16)


def fold3(y):
    n = y.shape[0] // 3
    return (y[2 * n :] + y[n : 2 * n]) + y[:n]


def dot(a, b):
    return lax.dot_general(a, b, (((1,), (0,)), ((), ())), preferred_element_type=F32)


def dot_nt(a, b):
    return lax.dot_general(a, b, (((1,), (1,)), ((), ())), preferred_element_type=F32)


WIDE = 256


def pick(values, index):
    rows, count = values.shape
    width = min(count, WIDE)
    parts = count // width
    stacked = jnp.concatenate([values[:, h * width : (h + 1) * width] for h in range(parts)], axis=0)
    found = fold3(dot(split3(stacked), onehot(width, index & (width - 1))))
    high = index >> (width.bit_length() - 1)
    result = found[:rows]
    for h in range(1, parts):
        result = jnp.where(high == h, found[h * rows : (h + 1) * rows], result)
    return result


def put(values, index, count):
    rows = 3 * values.shape[0]
    width = min(count, WIDE)
    parts = count // width
    high = index >> (width.bit_length() - 1)
    values = thirds(values)
    if parts > 1:
        values = jnp.concatenate([jnp.where(high == h, values, 0.0) for h in range(parts)], axis=0)
    sums = dot_nt(values.astype(BF16), onehot(width, index & (width - 1)))
    return jnp.concatenate([fold3(sums[h * rows : (h + 1) * rows]) for h in range(parts)], axis=1)


def onehot(count, index):
    hit = iota((count, index.shape[1]), 0) == index
    return jnp.where(hit, 1.0, 0.0).astype(BF16)


def pad_rows(x, n):
    return jnp.concatenate([x, jnp.zeros((n - x.shape[0], x.shape[1]), F32)], axis=0)


def row_parts(shape):
    row = iota(shape, 0)
    upper = (row >= 8).astype(I32)
    held = (row - 8 * upper) < ROWS // 2
    c = row - 2 * upper
    return held, c >> 2, c & (KB - 1)


def halves(x, low):
    return jnp.where(low, x[:8], x[8:])


def fetch(sources, targets, semaphores):
    copies = [pltpu.make_async_copy(a, b, semaphores.at[k]) for k, (a, b) in enumerate(zip(sources, targets))]
    for copy in copies:
        copy.start()
    return copies


def before_kernel(groups, slabs, *refs):
    sources, (send, partial_out, own), targets, semaphores = refs[:13], refs[13:16], refs[16:29], refs[29]
    order = [*range(7), 11, 12, *range(7, 11)]
    copies = fetch([sources[k] for k in order], [targets[k] for k in order], semaphores)
    for copy in copies[:9]:
        copy.wait()
    fill, recurrence, source_index, source_coeffs, source_vector, left, knot_coeffs, band, knots = (
        *targets[-2:],
        *targets[:7],
    )
    buckets, capacity = left.shape
    source_dev = source_vector.shape[1]
    knot_dev = knots.shape[2]
    bands = knot_dev // KB
    shift = bands.bit_length() - 1
    alpha = recurrence[0]
    low8 = iota((8, LANES), 1) < bands
    slot = iota((1, capacity), 1)

    my_slab = lax.axis_index("tm")
    total = jnp.zeros((groups, 1), F32)
    before = jnp.where(iota((capacity, capacity), 0) < iota((capacity, capacity), 1), 1.0, 0.0).astype(BF16)
    targets, columns = [], []
    for i in range(buckets):
        bands_i = band[pl.ds(i, 1), :]
        owner = bands_i >> shift
        named = jnp.where(iota((groups, capacity), 0) == owner, 1.0, 0.0)
        count = dot(named.astype(BF16), before) + total
        rank = jnp.sum(named * count, axis=0, keepdims=True).astype(I32)
        total = total + jnp.sum(named, axis=1, keepdims=True)
        targets.append(owner * bands + rank)
    index = jnp.concatenate([source_index[pl.ds(t, 1), :] for t in range(buckets)], axis=1)
    picked = pick(pad_rows(source_vector[...], 8), index)[:5]
    partial = []
    for t in range(buckets):
        image = jnp.sum(source_coeffs[:, t, :] * picked[:, t * capacity : (t + 1) * capacity], axis=0, keepdims=True)
        partial.append(jnp.where(slot < fill[t], image - alpha * left[pl.ds(t, 1), :], 0.0))
        partial_out[pl.ds(t, 1), :] = partial[t]

    zero = jnp.zeros((1, capacity), F32)
    for i in range(buckets):
        local = (band[pl.ds(i, 1), :] & (bands - 1)).astype(F32)
        place = (slot + i * capacity).astype(F32)
        here = my_slab == i
        coeffs = jnp.where(here & (slot >= fill[i]), 0.0, knot_coeffs[:, i, :])
        known = jnp.where(here, partial[i], 0.0)
        columns.append(
            jnp.concatenate([coeffs[: ROWS // 2], local, known, coeffs[ROWS // 2 :], place, zero], axis=0)
        )
    packed = put(jnp.concatenate(columns, axis=1), jnp.concatenate(targets, axis=1), groups * bands)

    held, axis_of, offset = row_parts((16, knot_dev))
    spread = jnp.zeros((16, knot_dev), F32)
    for a in range(3):
        spread = jnp.where(axis_of == a, knots[a], spread)
    spread = jnp.where(held & ((iota((16, knot_dev), 1) & (KB - 1)) == offset), spread, 0.0)
    hit = (iota((knot_dev, LANES), 0) >> 2) == (iota((knot_dev, LANES), 1) & (bands - 1))
    rows = fold3(dot(split3(spread), jnp.where(hit, 1.0, 0.0).astype(BF16)))
    own[0:16, :] = rows
    row, lane = iota((own.shape[0] - 16, LANES), 0), iota((own.shape[0] - 16, LANES), 1)
    scalars = jnp.where(lane == 0, alpha, jnp.where(lane == 1, recurrence[1], recurrence[2]))
    for t in range(buckets):
        scalars = jnp.where(row == 1 + t, fill[t].astype(F32), scalars)
    own[16:, :] = scalars
    knot_rows = halves(rows, low8)[: ROWS // 2]

    other = [
        jnp.concatenate(
            [partial[t][:, k * LANES : (k + 1) * LANES] for k in range(capacity // LANES)]
            + [jnp.full((8 - capacity // LANES, LANES), fill[t].astype(F32))],
            axis=0,
        )
        for t in range(buckets)
    ]
    for g in range(groups // 2):
        tile = packed[:, g * LANES : (g + 1) * LANES]
        turned = pltpu.roll(tile, bands, 1)
        pair = (jnp.where(low8, tile[:8], turned[8:]), jnp.where(low8, turned[:8], tile[8:]))
        for h in range(2):
            for t in range(slabs):
                row = (t * groups + 2 * g + h) * BLOCK
                send[row : row + 8, :] = jnp.where(my_slab == t, pair[h], other[t])
                send[row + 8 : row + BLOCK, :] = knot_rows
    for copy in copies[9:]:
        copy.wait()


def joined(even, odd, low, bands):
    return jnp.concatenate(
        [jnp.where(low, even, pltpu.roll(odd, bands, 1)), jnp.where(low, pltpu.roll(even, bands, 1), odd)], axis=0
    )


def middle_kernel(groups, slabs, recv, partial, left, source_index, source_coeffs, source_vector, knots, own, *refs):
    buckets, capacity = left.shape
    source_dev = source_vector.shape[1]
    knot_dev = knots.shape[2]
    bands = knot_dev // KB
    shift = bands.bit_length() - 1
    capacity_shift = capacity.bit_length() - 1
    devices = groups * slabs
    packets = groups * bands
    alpha = own[16:17, 0:1]
    my_slab = lax.axis_index("tm")
    moved, (raw_out, gradient_source, gradient_knot, sums) = refs[: 2 * slabs], refs[2 * slabs :]
    low = iota((8, LANES), 1) < bands
    slot = iota((1, capacity), 1).astype(F32)

    def blocks(t, start):
        rows = [(t * groups + s) * BLOCK + start for s in range(groups)]
        loaded = [recv[row : row + 8, :] for row in rows]
        return jnp.concatenate([joined(*loaded[k : k + 2], low, bands) for k in range(0, groups, 2)], axis=1)

    def of_slab(t, values):
        result = values[0]
        for k in range(1, slabs):
            result = jnp.where(my_slab == (t + k) % slabs, values[k], result)
        return result


    indices, weighted = [], []
    squares = jnp.zeros((1, capacity), F32)
    cross = jnp.zeros((1, capacity), F32)
    coeffs_of = [moved[2 * k][:, my_slab, :] for k in range(slabs)]
    bands_of = [moved[2 * k + 1][pl.ds(my_slab, 1), :] for k in range(slabs)]
    gap = jnp.zeros((2, capacity), F32)
    for t in range(slabs):
        block = of_slab(t, coeffs_of)
        coeffs = jnp.concatenate([gap, block[: ROWS // 2], gap, block[ROWS // 2 :]], axis=0)
        found = pick(blocks(t, 6), of_slab(t, bands_of))
        image = jnp.sum(coeffs * found, axis=0, keepdims=True)
        raw = partial[pl.ds(t, 1), :] + jnp.where(slot < own[pl.ds(17 + t, 1), 0:1], image, 0.0)
        raw_out[pl.ds(t, 1), :] = raw
        squares = squares + raw * raw
        cross = cross + raw * (raw + alpha * left[pl.ds(t, 1), :])
        indices.append(source_index[pl.ds(t, 1), :])
        weighted.append(pad_rows(source_coeffs[:, t, :] * raw, 8))
    packet = blocks(0, 0)
    for t in range(1, slabs):
        packet = jnp.where(my_slab == t, blocks(t, 0), packet)
    band = packet[6:7].astype(I32)
    place = packet[14:15].astype(I32)
    inner = place & (capacity - 1)
    first = place >> capacity_shift
    senders = WIDE // bands
    member = senders * slabs
    row = iota((member, WIDE), 0)
    sender = iota((1, WIDE), 1) >> shift
    found = []
    for q in range(packets // WIDE):
        lanes = slice(q * WIDE, (q + 1) * WIDE)
        part = [
            jnp.concatenate(
                [recv[pl.ds((i * groups + q * senders) * BLOCK + k, senders, stride=BLOCK), :] for i in range(slabs)],
                axis=0,
            )
            for k in range(capacity // LANES + 1)
        ]
        chosen = row == first[:, lanes] * senders + sender
        values = pick(jnp.concatenate(part[:-1], axis=1), inner[:, lanes])
        fills = jnp.concatenate([part[-1]] * (WIDE // LANES), axis=1)
        valid = jnp.sum(jnp.where(chosen, fills, 0.0), axis=0, keepdims=True)
        found.append((jnp.sum(jnp.where(chosen, values, 0.0), axis=0, keepdims=True), valid))
    partial_packet, fill_packet = (jnp.concatenate(x, axis=1) for x in zip(*found))
    image = jnp.sum(packet * pick(own[0:16, 0:bands], band), axis=0, keepdims=True)
    known = first == my_slab
    partial_packet = jnp.where(known, packet[7:8], partial_packet)
    packet_raw = jnp.where(known | (inner.astype(F32) < fill_packet), partial_packet + image, 0.0)
    hit = (iota((knot_dev, packets), 0) >> 2) == band
    spread = fold3(dot_nt(split3(packet * packet_raw), jnp.where(hit, 1.0, 0.0).astype(BF16)))
    held, axis_of, offset = row_parts((16, knot_dev))
    spread = jnp.where(held & ((iota((16, knot_dev), 1) & (KB - 1)) == offset), spread, 0.0)
    for a in range(3):
        gradient_knot[a] = jnp.sum(jnp.where(axis_of == a, spread, 0.0), axis=0, keepdims=True)

    gathered_sum = put(jnp.concatenate(weighted, axis=1), jnp.concatenate(indices, axis=1), source_dev)
    gradient_source[...] = gathered_sum[:5]
    def across(x):
        x = jnp.sum(x, axis=0, keepdims=True)
        return functools.reduce(jnp.add, [x[:, k : k + LANES] for k in range(0, x.shape[1], LANES)])

    old = source_vector[...]
    old_knots = sum(knots[a] * knots[a] for a in range(3))
    new_knots = sum(gradient_knot[a] * gradient_knot[a] for a in range(3))
    parts = (
        across(squares),
        across(gathered_sum * gathered_sum) + across(new_knots),
        across(cross),
        across(old * old) + across(old_knots),
    )
    quarter = iota((8, LANES), 0)
    stacked = jnp.zeros((8, LANES), F32)
    for k, part in enumerate(parts):
        stacked = jnp.where(quarter == k, part, stacked)
    totals = jnp.where(quarter == iota((8, LANES), 1), jnp.sum(stacked, axis=1, keepdims=True), 0.0)
    sums[...] = jnp.broadcast_to(jnp.sum(totals, axis=0, keepdims=True), sums.shape)


def after_kernel(total_obs, unknowns, sums, own, raw, gradient_source, gradient_knot, source_vector, knots, source_search, knot_search, source_solution, knot_solution, left_next, source_next, knot_next, search_source, search_knot, solution_source, solution_knot, recurrence_next):
    ratio = unknowns / total_obs
    pivot, remainder = own[16:17, 1:2], own[16:17, 2:3]
    total = jnp.sum(sums[...], axis=0, keepdims=True)
    s0, s1, s2, s3 = (total[:, k : k + 1] for k in range(4))
    beta = jnp.sqrt(s0 / total_obs + EPSILON)
    scaled = ratio / beta
    alpha_square = scaled * scaled * s1 - 2.0 * ratio * s2 + beta * beta * s3
    alpha_next = jnp.sqrt(alpha_square / unknowns + EPSILON)
    radius = jnp.sqrt(pivot * pivot + beta * beta)
    cosine = pivot / radius
    sine = beta / radius
    gain = cosine * remainder / radius
    turn = sine * alpha_next / radius
    one_gradient = scaled / alpha_next
    one_vector = beta / alpha_next
    left_next[...] = raw[...] / beta
    search = source_search[...]
    value = one_gradient * gradient_source[...] - one_vector * source_vector[...]
    source_next[...] = value
    search_source[...] = value - turn * search
    solution_source[...] = source_solution[...] + gain * search
    for a in range(3):
        search = knot_search[a]
        value = one_gradient * gradient_knot[a] - one_vector * knots[a]
        knot_next[a] = value
        search_knot[a] = value - turn * search
        solution_knot[a] = knot_solution[a] + gain * search
    for k, value in enumerate((alpha_next, beta, -cosine * alpha_next, sine * remainder)):
        recurrence_next[k] = value[0, 0]


VMEM = pl.BlockSpec(memory_space=pltpu.VMEM)
SMEM = pl.BlockSpec(memory_space=pltpu.SMEM)
HBM = pl.BlockSpec(memory_space=pltpu.HBM)


def shards(
    left_vector,
    source_coeffs,
    knot_coeffs,
    source_index,
    band_start,
    bucket_fill,
    source_vector,
    knot_vector,
    source_search,
    knot_search,
    source_solution,
    knot_solution,
    recurrence,
):
    slabs = lax.axis_size("tm")
    groups = lax.axis_size("src")
    devices = slabs * groups
    buckets, capacity = left_vector.shape
    source_dev = source_vector.shape[1]
    knot_dev = knot_vector.shape[2]
    total_obs = buckets * capacity * devices
    unknowns = (5 * source_dev + 3 * knot_dev) * devices
    params = pltpu.CompilerParams(vmem_limit_bytes=48 * 1024 * 1024)
    shape = jax.ShapeDtypeStruct

    fill = bucket_fill.reshape(-1)
    operands = (
        source_index,
        source_coeffs,
        source_vector,
        left_vector,
        knot_coeffs,
        band_start,
        knot_vector,
        source_search,
        knot_search,
        source_solution,
        knot_solution,
        fill,
        recurrence,
    )
    send, partial, own, *held = pl.pallas_call(
        functools.partial(before_kernel, groups, slabs),
        out_shape=(
            shape((devices * BLOCK, LANES), F32),
            shape((buckets, capacity), F32),
            shape((16 + 8 * pl.cdiv(1 + buckets, 8), LANES), F32),
            *(pltpu.VMEM(x.shape, x.dtype) for x in operands[:-2]),
        ),
        in_specs=[HBM] * len(operands),
        out_specs=(VMEM,) * 14,
        scratch_shapes=[pltpu.SMEM(x.shape, x.dtype) for x in operands[-2:]]
        + [pltpu.SemaphoreType.DMA((len(operands),))],
        compiler_params=params,
        name="before",
    )(*(pltpu.with_memory_space_constraint(x, pltpu.HBM) for x in operands))
    source_index, source_coeffs, source_vector, left_held, knot_coeffs, band_start, knots_held, *later = held
    moved = []
    for k in range(1, slabs):
        shifted = [(t, (t + k) % slabs) for t in range(slabs)]
        moved += [lax.ppermute(knot_coeffs, "tm", shifted), lax.ppermute(band_start, "tm", shifted)]

    send = send.reshape(devices * BLOCK, 1, LANES)
    recv = lax.all_to_all(send, ("tm", "src"), split_axis=0, concat_axis=0, tiled=True)
    recv = recv.reshape(devices * BLOCK, LANES)
    raw, gradient_source, gradient_knot, sums = pl.pallas_call(
        functools.partial(middle_kernel, groups, slabs),
        out_shape=(
            shape((buckets, capacity), F32),
            shape((5, source_dev), F32),
            shape((3, 1, knot_dev), F32),
            shape((devices, LANES), F32),
        ),
        in_specs=[VMEM] * (8 + 2 * slabs),
        out_specs=(VMEM,) * 4,
        compiler_params=params,
        name="middle",
    )(
        recv,
        partial,
        left_held,
        source_index,
        source_coeffs,
        source_vector,
        knots_held,
        own,
        knot_coeffs,
        band_start,
        *moved,
    )
    sums = lax.all_to_all(sums, ("tm", "src"), split_axis=0, concat_axis=0, tiled=True)
    like = [shape(x.shape, F32) for x in (left_vector, source_vector, knot_vector)]
    outs = pl.pallas_call(
        functools.partial(after_kernel, total_obs, unknowns),
        out_shape=(like[0], like[1], like[2], like[1], like[2], like[1], like[2], shape((4,), F32)),
        in_specs=[VMEM] * 11,
        out_specs=(VMEM,) * 7 + (SMEM,),
        compiler_params=params,
        name="after",
    )(
        sums,
        own,
        raw,
        gradient_source,
        gradient_knot,
        source_vector,
        knots_held,
        *later,
    )
    return outs


def solution(mesh):
    wide = ("src", "tm")
    flat = P(None, wide)
    knot = P(None, "tm", "src")
    in_specs = (flat, P(None, None, wide), P(None, None, wide), flat, flat, flat, flat, knot, flat, knot, flat, knot, P())
    out_specs = (flat, flat, knot, flat, knot, flat, knot, P())
    return jax.shard_map(shards, mesh=mesh, in_specs=in_specs, out_specs=out_specs, check_vma=False)
```
